32 devices in a mesh: fsdp: 16 (over z, y, x), dp: 2 (over core).
Axes of the slice: x: 2, y: 2, z: 4, core: 2. Of those that a mesh axis runs over, the one named last changes fastest.
Arguments:
- tokens: bfloat16 [2, 32768, 640], P(None, ('fsdp', 'dp')), may hold values from -6 to 6
- cotangent: bfloat16 [2, 32768, 640], P(None, ('fsdp', 'dp')), may hold values from -6 to 6
- seq_lengths: int32 [64], replicated, may hold values from 256 to 1024, as said below
- slot_of: int32 [64], replicated, may hold values from 0 to 63, each once
- w_query: bfloat16 [640, 1024], P('fsdp'), may hold values from -0.25 to 0.25
- w_key: bfloat16 [640, 256], P('fsdp'), may hold values from -0.25 to 0.25
- w_value: bfloat16 [640, 256], P('fsdp'), may hold values from -0.25 to 0.25
- w_out: bfloat16 [1024, 640], P(None, 'fsdp'), may hold values from -0.1875 to 0.1875
- w_gate: bfloat16 [640, 2048], P('fsdp'), may hold values from -0.25 to 0.25
- w_up: bfloat16 [640, 2048], P('fsdp'), may hold values from -0.25 to 0.25
- w_down: bfloat16 [2048, 640], P(None, 'fsdp'), may hold values from -0.125 to 0.125
- gain_attn_in: bfloat16 [640], P('fsdp'), may hold values from 0.25 to 1.75
- gain_query: bfloat16 [256], P('fsdp'), may hold values from 0.25 to 1.75
- gain_key: bfloat16 [256], P('fsdp'), may hold values from 0.25 to 1.75
- gain_attn_out: bfloat16 [640], P('fsdp'), may hold values from 0.25 to 1.75
- gain_ffn_in: bfloat16 [640], P('fsdp'), may hold values from 0.25 to 1.75
- gain_ffn_out: bfloat16 [640], P('fsdp'), may hold values from 0.25 to 1.75
Outputs:
- activations: bfloat16 [2, 32768, 640], P(None, ('fsdp', 'dp'))
- input_grad: bfloat16 [2, 32768, 640], P(None, ('fsdp', 'dp'))
- grad_w_query: float32 [640, 1024], P('fsdp')
- grad_w_key: float32 [640, 256], P('fsdp')
- grad_w_value: float32 [640, 256], P('fsdp')
- grad_w_out: float32 [1024, 640], P(None, 'fsdp')
- grad_w_gate: float32 [640, 2048], P('fsdp')
- grad_w_up: float32 [640, 2048], P('fsdp')
- grad_w_down: float32 [2048, 640], P(None, 'fsdp')
- grad_gain_attn_in: float32 [640], P('fsdp')
- grad_gain_query: float32 [256], P('fsdp')
- grad_gain_key: float32 [256], P('fsdp')
- grad_gain_attn_out: float32 [640], P('fsdp')
- grad_gain_ffn_in: float32 [640], P('fsdp')
- grad_gain_ffn_out: float32 [640], P('fsdp')
The draws below stay inside these ranges and needn't reach their ends.
Inputs may be any that keep to these rules, and one draw needn't show every extreme that they name: seq_lengths[p] tokens of sequence p are real, the rest of its slot is padding; some sequence has exactly 1024 tokens. `slot_of`: every slot holds exactly one sequence.
All inputs are finite; a program needn't handle non-finite values.
Results may differ from the reference program's by a relative error of at most 0.018.
Values may be sent and summed in bfloat16 or wider, within the bound.
No kernel may reach another device: no remote copies, remote signals or barrier semaphores. Data moves between devices by JAX's collectives and lax.ppermute only.
A program may use at most 192 MiB of HBM per device.

```python
import math
import jax
import jax.numpy as jnp
from jax import lax

D = 640
HEADS = 4
HD = 256
FF = 2048
W = 512
MB = 2
SLOT = 1024
LEN_MIN = 256
SLOTS = 64
TOKENS = 32768
N_FSDP = 16
N_DP = 2


def draw_seq_lengths(key, part):
    key = jax.random.fold_in(key, 11)
    first, second = jax.random.split(key)
    values = jax.random.randint(first, (SLOTS,), LEN_MIN, SLOT + 1)
    spot = jax.random.randint(second, (), 0, SLOTS)
    return jnp.where(jnp.arange(SLOTS) == spot, SLOT, values).astype(jnp.int32)


def with_spikes(values, stream_key, source, target, parts, factor):
    def block_of(dim):
        return (jnp.arange(values.shape[dim]) // (values.shape[dim] // parts)).reshape((-1,) + (1,) * (values.ndim - 1 - dim))

    first = jax.random.permutation(stream_key, parts)[block_of(target)]
    other_side = (block_of(target) + parts // 2) % parts
    return jnp.where((block_of(source) == first) | (block_of(source) == other_side), factor * values, values)


def steps_of(rng, shape, cuts, smallest, largest):
    level, own = 1.0, jax.random.fold_in(rng, 6)
    for axis_at, blocks in cuts:
        draws = jnp.exp(jax.random.uniform(jax.random.fold_in(own, axis_at), (blocks,), jnp.float32, smallest / len(cuts), largest / len(cuts)))
        level = level * jnp.repeat(draws, shape[axis_at] // blocks).reshape([-1 if axis == axis_at else 1 for axis in range(len(shape))])
    return level


def scatter_about(stream_key, dims, deviation, reach, shards=(), held_as=jnp.bfloat16):
    factor_of = steps_of(stream_key, dims, shards, -0.22, 0.18) if shards else 1.0
    array = jax.random.normal(stream_key, dims, jnp.float32) * deviation * factor_of
    return jnp.minimum(jnp.maximum(array, -reach), reach).astype(held_as)


def gaussian_with(own_key, shape, deviation, bound, cuts, heavy, kind=jnp.bfloat16):
    entries = deviation * jax.random.normal(own_key, shape, jnp.float32)
    if cuts:
        entries = entries * steps_of(own_key, shape, cuts, -0.22, 0.18)
    return jnp.clip(with_spikes(entries, jax.random.fold_in(own_key, 3), *heavy), -bound, bound).astype(kind)


def setup_inputs(seed: int = 0) -> dict:
    splits = jax.random.split(jax.random.key(seed), 18)
    tokens = gaussian_with(splits[0], (MB, TOKENS, D), 1.0, 6.0, ((1, 32),), (1, 2, 32, 2.75))
    cotangent = gaussian_with(splits[1], (MB, TOKENS, D), 1.0, 6.0, ((1, 32),), (1, 2, 32, 2.75))
    seq_lengths = draw_seq_lengths(jax.random.fold_in(splits[17], 71), 0)
    slot_of = jax.random.permutation(splits[3], SLOTS).astype(jnp.int32)
    w_query = scatter_about(splits[4], (D, HEADS * HD), D ** -0.5, 0.25, ((0, 16),))
    w_key = scatter_about(splits[5], (D, HD), D ** -0.5, 0.25, ((0, 16),))
    w_value = scatter_about(splits[6], (D, HD), D ** -0.5, 0.25, ((0, 16),))
    w_out = scatter_about(splits[7], (HEADS * HD, D), (HEADS * HD) ** -0.5, 0.1875, ((1, 16),))
    w_gate = scatter_about(splits[8], (D, FF), D ** -0.5, 0.25, ((0, 16),))
    w_up = scatter_about(splits[9], (D, FF), D ** -0.5, 0.25, ((0, 16),))
    w_down = scatter_about(splits[10], (FF, D), FF ** -0.5, 0.125, ((1, 16),))
    gain_attn_in = jnp.clip(1.0 + 0.15 * jax.random.normal(splits[11], (D,), jnp.float32), 0.25, 1.75).astype(jnp.bfloat16)
    gain_query = jnp.clip(1.0 + 0.15 * jax.random.normal(splits[12], (HD,), jnp.float32), 0.25, 1.75).astype(jnp.bfloat16)
    gain_key = jnp.clip(1.0 + 0.15 * jax.random.normal(splits[13], (HD,), jnp.float32), 0.25, 1.75).astype(jnp.bfloat16)
    gain_attn_out = jnp.clip(1.0 + 0.15 * jax.random.normal(splits[14], (D,), jnp.float32), 0.25, 1.75).astype(jnp.bfloat16)
    gain_ffn_in = jnp.clip(1.0 + 0.15 * jax.random.normal(splits[15], (D,), jnp.float32), 0.25, 1.75).astype(jnp.bfloat16)
    gain_ffn_out = jnp.clip(1.0 + 0.15 * jax.random.normal(splits[16], (D,), jnp.float32), 0.25, 1.75).astype(jnp.bfloat16)
    return dict(tokens=tokens, cotangent=cotangent, seq_lengths=seq_lengths, slot_of=slot_of, w_query=w_query, w_key=w_key, w_value=w_value, w_out=w_out, w_gate=w_gate, w_up=w_up, w_down=w_down, gain_attn_in=gain_attn_in, gain_query=gain_query, gain_key=gain_key, gain_attn_out=gain_attn_out, gain_ffn_in=gain_ffn_in, gain_ffn_out=gain_ffn_out)


norm_eps = 1e-06
rope_base = 10000.0
masked_fill = -1e+30
highest = lax.Precision.HIGHEST

@jax.custom_vjp
def low(v):
    return lax.optimization_barrier(v.astype(jnp.bfloat16)).astype(jnp.float32)

@jax.custom_vjp
def low_back(v):
    return v

def low_keep(v):
    return (low(v), None)

def low_pass(kept, grad):
    return (grad,)

def back_keep(v):
    return (v, None)

def back_low(kept, grad):
    return (low(grad),)
low.defvjp(low_keep, low_pass)
low_back.defvjp(back_keep, back_low)

def rms_scale(value, gain):
    return value * lax.rsqrt(lax.optimization_barrier(jnp.mean(value * value, axis=-1, keepdims=True)) + norm_eps) * gain

def rotate(value, cosine, sine):
    half = value.shape[-1] // 2
    first = value[..., :half]
    second = value[..., half:]
    return jnp.concatenate([first * cosine - second * sine, second * cosine + first * sine], axis=-1)

def rope_tables(rows, head_dim):
    half = head_dim // 2
    inverse = 1.0 / rope_base ** (jnp.arange(half, dtype=jnp.float32) * 2.0 / head_dim)
    angle = jnp.arange(rows, dtype=jnp.float32)[:, None] * inverse[None, :]
    return (jnp.cos(angle), jnp.sin(angle))

def project(left, right):
    return jnp.einsum('gsd,de->gse', left, right, precision=highest)

def forward(inputs, params, valid, allowed):
    w_query, w_key, w_value, w_out, w_gate, w_up, w_down, gain_attn_in, gain_query, gain_key, gain_attn_out, gain_ffn_in, gain_ffn_out = params
    groups, rows, width = inputs.shape
    cosine, sine = rope_tables(rows, HD)
    normed = low(rms_scale(inputs, gain_attn_in))
    query_lin = low_back(project(normed, w_query)).reshape(groups, rows, HEADS, HD)
    key_lin = low_back(project(normed, w_key))
    value_rows = low(low_back(project(normed, w_value)))
    query_rot = low(rotate(rms_scale(query_lin, gain_query), cosine[:, None, :], sine[:, None, :]))
    key_rot = low(rotate(rms_scale(key_lin, gain_key), cosine, sine))
    scores = low_back(jnp.einsum('gqhd,gkd->ghqk', query_rot, key_rot, precision=highest) * HD ** (-0.5))
    masked = jnp.where(allowed[:, None], scores, masked_fill)
    top = lax.optimization_barrier(jnp.max(masked, axis=-1, keepdims=True))
    expon = jnp.exp(masked - top)
    probs = low(expon / lax.optimization_barrier(jnp.sum(expon, axis=-1, keepdims=True)))
    mixed = low(low_back(jnp.einsum('ghqk,gkd->gqhd', probs, value_rows, precision=highest)))
    mixed = mixed.reshape(groups, rows, HEADS * HD)
    attended = low_back(project(mixed, w_out))
    hidden_res = inputs + rms_scale(attended, gain_attn_out)
    ffn_in = low(rms_scale(hidden_res, gain_ffn_in))
    gate = low_back(project(ffn_in, w_gate))
    up_proj = low_back(project(ffn_in, w_up))
    inner = low(jax.nn.gelu(gate, approximate=True) * up_proj)
    result = low_back(project(inner, w_down))
    return valid[..., None] * (hidden_res + rms_scale(result, gain_ffn_out))

def reference(tokens, cotangent, seq_lengths, slot_of, w_query, w_key, w_value, w_out, w_gate, w_up, w_down, gain_attn_in, gain_query, gain_key, gain_attn_out, gain_ffn_in, gain_ffn_out):
    count = MB * N_FSDP * N_DP
    group = math.gcd(count, max(1, 4096 // SLOT))
    turns = count // group
    slot_len = jnp.zeros((count,), jnp.int32).at[slot_of.astype(jnp.int32)].set(seq_lengths.astype(jnp.int32))
    inputs = tokens.astype(jnp.float32).reshape(turns, group, SLOT, D)
    upstream = cotangent.astype(jnp.float32).reshape(turns, group, SLOT, D)
    lengths = slot_len.reshape(turns, group)
    params = tuple((piece.astype(jnp.float32) for piece in (w_query, w_key, w_value, w_out, w_gate, w_up, w_down, gain_attn_in, gain_query, gain_key, gain_attn_out, gain_ffn_in, gain_ffn_out)))
    positions = jnp.arange(SLOT, dtype=jnp.int32)
    query_pos = positions[:, None]
    key_pos = positions[None, :]

    def step(carry, item):
        batch, upper, length_group = item
        valid = (positions[None, :] < length_group[:, None]).astype(jnp.float32)
        window = (key_pos <= query_pos) & (query_pos - key_pos < W)
        allowed = window[None] & (key_pos[None] < length_group[:, None, None]) | (key_pos == query_pos)[None]

        def layer(batch_in, params_in):
            return forward(batch_in, params_in, valid, allowed)
        outputs, pull = jax.vjp(layer, batch, params)
        grad_in, grad_params = pull(upper)
        totals = tuple((old + new for old, new in zip(carry, grad_params)))
        return (totals, (outputs.astype(jnp.bfloat16), grad_in.astype(jnp.bfloat16)))
    start = tuple((jnp.zeros_like(piece) for piece in params))
    totals, (outputs, grads_in) = lax.scan(step, start, (inputs, upstream, lengths))
    activations = outputs.reshape(MB, SLOT * N_FSDP * N_DP, D)
    input_grad = grads_in.reshape(MB, SLOT * N_FSDP * N_DP, D)
    return (activations, input_grad, totals[0], totals[1], totals[2], totals[3], totals[4], totals[5], totals[6], totals[7], totals[8], totals[9], totals[10], totals[11], totals[12])
```

```python
import functools

import jax
import jax.numpy as jnp
from jax import lax
from jax.sharding import PartitionSpec as P

HEADS = 4
HD = 256
W = 512


norm_eps = 1e-06
rope_base = 10000.0
masked_fill = -1e30


def rms_scale(value, gain):
    return value * lax.rsqrt(jnp.mean(value * value, axis=-1, keepdims=True) + norm_eps) * gain


def rotate(value, cosine, sine):
    half = value.shape[-1] // 2
    first = value[..., :half]
    second = value[..., half:]
    return jnp.concatenate(
        [first * cosine - second * sine, second * cosine + first * sine], axis=-1
    )


def rope_tables(rows, head_dim):
    half = head_dim // 2
    inverse = 1.0 / rope_base ** (jnp.arange(half, dtype=jnp.float32) * 2.0 / head_dim)
    angle = jnp.arange(rows, dtype=jnp.float32)[:, None] * inverse[None, :]
    return (jnp.cos(angle), jnp.sin(angle))


def prepare(linear, gain, cosine, sine):
    return rotate(rms_scale(linear, gain), cosine, sine)


def activate(gate_in, up_in):
    return jax.nn.gelu(gate_in, approximate=True) * up_in


def left_trans(left, right):
    return lax.dot_general(
        left, right, (((0,), (0,)), ((), ())), preferred_element_type=jnp.float32
    )


def right_trans(left, right):
    return lax.dot_general(
        left, right, (((1,), (1,)), ((), ())), preferred_element_type=jnp.float32
    )


def key_mask(query_start, key_start, query_rows, key_rows, length):
    query_pos = query_start + jnp.arange(query_rows, dtype=jnp.int32)[:, None]
    key_pos = key_start + jnp.arange(key_rows, dtype=jnp.int32)[None, :]
    inside = (key_pos <= query_pos) & (query_pos - key_pos < W) & (key_pos < length)
    return inside | (key_pos == query_pos)


def unpack(params):
    gains = tuple((piece.astype(jnp.float32) for piece in params[7:]))
    return (params[:7], gains)


def block_scores(query_rot, key_rot, block, length):
    start = block * W
    key_start = max(0, start - W)
    stop = start + W
    scores = jnp.einsum(
        "qhd,kd->hqk",
        query_rot[start:stop],
        key_rot[key_start:stop],
        preferred_element_type=jnp.float32,
    ) * HD ** (-0.5)
    allowed = key_mask(start, key_start, W, stop - key_start, length)
    return (jnp.where(allowed[None], scores, masked_fill), start, key_start, stop)


def forward_pass(params, tokens_mb, length):
    matrices, gains = unpack(params)
    w_query, w_key, w_value, w_out, w_gate, w_up, w_down = matrices
    gain_attn_in, gain_query, gain_key, gain_attn_out, gain_ffn_in, gain_ffn_out = gains
    rows = tokens_mb.shape[0]
    cosine, sine = rope_tables(rows, HD)
    inputs = tokens_mb.astype(jnp.float32)
    normed = rms_scale(inputs, gain_attn_in).astype(jnp.bfloat16)
    query_lin = jnp.dot(normed, w_query, preferred_element_type=jnp.float32).reshape(
        rows, HEADS, HD
    )
    key_lin = jnp.dot(normed, w_key, preferred_element_type=jnp.float32)
    value_rows = jnp.dot(normed, w_value, preferred_element_type=jnp.float32).astype(jnp.bfloat16)
    query_rot = prepare(query_lin, gain_query, cosine[:, None, :], sine[:, None, :]).astype(
        jnp.bfloat16
    )
    key_rot = prepare(key_lin, gain_key, cosine, sine).astype(jnp.bfloat16)
    mixed_blocks = []
    lse_blocks = []
    for block in range(rows // W):
        masked, start, key_start, stop = block_scores(query_rot, key_rot, block, length)
        top = jnp.max(masked, axis=-1, keepdims=True)
        expon = jnp.exp(masked - top)
        total = jnp.sum(expon, axis=-1, keepdims=True)
        probs = (expon / total).astype(jnp.bfloat16)
        mixed_blocks.append(
            jnp.einsum(
                "hqk,kd->qhd", probs, value_rows[key_start:stop], preferred_element_type=jnp.float32
            ).astype(jnp.bfloat16)
        )
        lse_blocks.append(top + jnp.log(total))
    mixed = jnp.concatenate(mixed_blocks, axis=0).reshape(rows, HEADS * HD)
    attended = jnp.dot(mixed, w_out, preferred_element_type=jnp.float32)
    hidden_res = inputs + rms_scale(attended, gain_attn_out)
    ffn_in = rms_scale(hidden_res, gain_ffn_in).astype(jnp.bfloat16)
    gate = jnp.dot(ffn_in, w_gate, preferred_element_type=jnp.float32)
    up_proj = jnp.dot(ffn_in, w_up, preferred_element_type=jnp.float32)
    inner = activate(gate, up_proj).astype(jnp.bfloat16)
    result = jnp.dot(inner, w_down, preferred_element_type=jnp.float32)
    valid = (jnp.arange(rows, dtype=jnp.int32) < length).astype(jnp.float32)
    outputs = (valid[:, None] * (hidden_res + rms_scale(result, gain_ffn_out))).astype(jnp.bfloat16)
    kept = (
        inputs,
        normed,
        query_lin,
        key_lin,
        value_rows,
        query_rot,
        key_rot,
        tuple(lse_blocks),
        mixed,
        attended,
        hidden_res,
        ffn_in,
        gate,
        up_proj,
        inner,
        result,
        valid,
    )
    return (kept, outputs)


def backward_pass(params, kept, cot_mb, length):
    matrices, gains = unpack(params)
    w_query, w_key, w_value, w_out, w_gate, w_up, w_down = matrices
    gain_attn_in, gain_query, gain_key, gain_attn_out, gain_ffn_in, gain_ffn_out = gains
    (
        inputs,
        normed,
        query_lin,
        key_lin,
        value_rows,
        query_rot,
        key_rot,
        lse_blocks,
        mixed,
        attended,
        hidden_res,
        ffn_in,
        gate,
        up_proj,
        inner,
        result,
        valid,
    ) = kept
    rows = cot_mb.shape[0]
    cosine, sine = rope_tables(rows, HD)
    upstream = valid[:, None] * cot_mb.astype(jnp.float32)
    _, pull = jax.vjp(rms_scale, result, gain_ffn_out)
    grad_result, grad_gain_ffn_out = pull(upstream)
    grad_result = grad_result.astype(jnp.bfloat16)
    grad_w_down = left_trans(inner, grad_result)
    grad_inner = right_trans(grad_result, w_down)
    _, pull = jax.vjp(activate, gate, up_proj)
    grad_gate, grad_up = pull(grad_inner)
    grad_gate = grad_gate.astype(jnp.bfloat16)
    grad_up = grad_up.astype(jnp.bfloat16)
    grad_w_gate = left_trans(ffn_in, grad_gate)
    grad_w_up = left_trans(ffn_in, grad_up)
    grad_ffn_in = right_trans(grad_gate, w_gate) + right_trans(grad_up, w_up)
    _, pull = jax.vjp(rms_scale, hidden_res, gain_ffn_in)
    grad_hidden, grad_gain_ffn_in = pull(grad_ffn_in)
    grad_hidden = upstream + grad_hidden
    _, pull = jax.vjp(rms_scale, attended, gain_attn_out)
    grad_attended, grad_gain_attn_out = pull(grad_hidden)
    grad_attended = grad_attended.astype(jnp.bfloat16)
    grad_w_out = left_trans(mixed, grad_attended)
    grad_mixed = right_trans(grad_attended, w_out).astype(jnp.bfloat16).reshape(rows, HEADS, HD)
    query_parts = []
    grad_key_rot = jnp.zeros((rows, HD), jnp.float32)
    grad_value = jnp.zeros((rows, HD), jnp.float32)
    for block in range(rows // W):
        masked, start, key_start, stop = block_scores(query_rot, key_rot, block, length)
        probs = jnp.exp(masked - lse_blocks[block])
        grad_block = grad_mixed[start:stop]
        grad_value = grad_value.at[key_start:stop].add(
            jnp.einsum(
                "hqk,qhd->kd",
                probs.astype(jnp.bfloat16),
                grad_block,
                preferred_element_type=jnp.float32,
            )
        )
        grad_probs = jnp.einsum(
            "qhd,kd->hqk",
            grad_block,
            value_rows[key_start:stop],
            preferred_element_type=jnp.float32,
        )
        row_dot = jnp.sum(probs * grad_probs, axis=-1, keepdims=True)
        grad_scores = (probs * (grad_probs - row_dot)).astype(jnp.bfloat16)
        query_parts.append(
            jnp.einsum(
                "hqk,kd->qhd",
                grad_scores,
                key_rot[key_start:stop],
                preferred_element_type=jnp.float32,
            )
            * HD ** (-0.5)
        )
        grad_key_rot = grad_key_rot.at[key_start:stop].add(
            jnp.einsum(
                "hqk,qhd->kd",
                grad_scores,
                query_rot[start:stop],
                preferred_element_type=jnp.float32,
            )
            * HD ** (-0.5)
        )
    grad_query_rot = jnp.concatenate(query_parts, axis=0)
    grad_value = grad_value.astype(jnp.bfloat16)

    def query_piece(linear, gain):
        return prepare(linear, gain, cosine[:, None, :], sine[:, None, :])

    def key_piece(linear, gain):
        return prepare(linear, gain, cosine, sine)

    _, pull = jax.vjp(query_piece, query_lin, gain_query)
    grad_query_lin, grad_gain_query = pull(grad_query_rot)
    grad_query_lin = grad_query_lin.reshape(rows, HEADS * HD).astype(jnp.bfloat16)
    _, pull = jax.vjp(key_piece, key_lin, gain_key)
    grad_key_lin, grad_gain_key = pull(grad_key_rot)
    grad_key_lin = grad_key_lin.astype(jnp.bfloat16)
    grad_w_query = left_trans(normed, grad_query_lin)
    grad_w_key = left_trans(normed, grad_key_lin)
    grad_w_value = left_trans(normed, grad_value)
    grad_normed = (
        right_trans(grad_query_lin, w_query)
        + right_trans(grad_key_lin, w_key)
        + right_trans(grad_value, w_value)
    )
    _, pull = jax.vjp(rms_scale, inputs, gain_attn_in)
    grad_inputs, grad_gain_attn_in = pull(grad_normed)
    input_grad = (grad_hidden + grad_inputs).astype(jnp.bfloat16)
    grads = (
        grad_w_query,
        grad_w_key,
        grad_w_value,
        grad_w_out,
        grad_w_gate,
        grad_w_up,
        grad_w_down,
        grad_gain_attn_in,
        grad_gain_query,
        grad_gain_key,
        grad_gain_attn_out,
        grad_gain_ffn_in,
        grad_gain_ffn_out,
    )
    return (input_grad, grads)


def factors(count):
    side = 1
    while 2 * side**3 < count:
        side += 1
    return (2 * side, side, side) if 2 * side**3 == count else (count, 1, 1)


def place(sizes, axis):
    index = lax.axis_index("fsdp")
    for size in sizes[axis + 1 :]:
        index = index // size
    return index % sizes[axis]


def shifted(sizes, axis, step):
    stride = 1
    for size in sizes[axis + 1 :]:
        stride *= size
    pairs = []
    for index in range(sizes[0] * sizes[1] * sizes[2]):
        at = (index // stride) % sizes[axis]
        pairs.append((index, index + ((at + step) % sizes[axis] - at) * stride))
    return pairs


def gather_axis(block, sizes, axis, at):
    size = sizes[axis]
    if size == 1:
        return jnp.expand_dims(block, at)
    here = place(sizes, axis)
    pieces = [block] + [
        lax.ppermute(block, "fsdp", shifted(sizes, axis, step)) for step in range(1, size)
    ]
    if size == 2:
        own, other = pieces
        low = here == 0
        return jnp.stack([jnp.where(low, own, other), jnp.where(low, other, own)], axis=at)
    out = jnp.zeros(block.shape[:at] + (size,) + block.shape[at:], block.dtype)
    for step, piece in enumerate(pieces):
        out = lax.dynamic_update_slice_in_dim(
            out, jnp.expand_dims(piece, at), (here - step) % size, at
        )
    return out


def gather_rows(block, cut, sizes):
    rows = block.shape[0] * sizes[0] * sizes[1] * sizes[2]
    part = gather_axis(block, sizes, 0, 0)
    first = gather_axis(gather_axis(part[..., :cut], sizes, 1, 1), sizes, 2, 2)
    second = gather_axis(gather_axis(part[..., cut:], sizes, 2, 1), sizes, 1, 1)
    return first.reshape(rows, -1), second.reshape(rows, -1)


def swap(block):
    return lax.ppermute(block, "dp", [(0, 1), (1, 0)])


def total(parts):
    out = parts[0].astype(jnp.float32)
    for part in parts[1:]:
        out = out + part.astype(jnp.float32)
    return out


def pick(parts, index, at):
    return [lax.dynamic_index_in_dim(part, index, at, keepdims=False) for part in parts]


def reduce_axis(parts, sizes, axis, at):
    size = sizes[axis]
    here = place(sizes, axis)
    arrived = [
        lax.ppermute(
            total(pick(parts, (here + step) % size, at)).astype(jnp.bfloat16),
            "fsdp",
            shifted(sizes, axis, step),
        )
        for step in range(1, size)
    ]
    return pick(parts, here, at) + arrived


def reduce_rows(mine, theirs, sizes, flip):
    box = sizes + (mine.shape[0] // (sizes[0] * sizes[1] * sizes[2]), mine.shape[1])
    parts = [mine.reshape(box), swap(theirs).reshape(box)]
    if flip:
        parts = reduce_axis(reduce_axis(parts, sizes, 1, 1), sizes, 2, 1)
    else:
        parts = reduce_axis(reduce_axis(parts, sizes, 2, 2), sizes, 1, 1)
    return total(reduce_axis(parts, sizes, 0, 0))


def half_of(array, core, axis):
    size = array.shape[axis] // 2
    return lax.dynamic_slice_in_dim(array, core * size, size, axis)


def in_order(core, mine, theirs):
    return jnp.concatenate([jnp.where(core == 0, mine, theirs), jnp.where(core == 0, theirs, mine)], axis=1)


def pack_gains(pieces, rows):
    columns = [jnp.pad(piece, (0, rows - piece.shape[0])) for piece in pieces]
    return jnp.pad(jnp.stack(columns, axis=1), ((0, 0), (0, 128 - len(columns))))


def pack_gain_grads(pieces, count, rows):
    columns = [
        jnp.pad(piece.reshape(count, -1), ((0, 0), (0, rows - piece.shape[0] // count))).reshape(-1)
        for piece in pieces
    ]
    return jnp.pad(jnp.stack(columns, axis=1), ((0, 0), (0, 128 - len(columns))))


def local(
    sizes,
    tokens,
    cotangent,
    seq_lengths,
    slot_of,
    w_query,
    w_key,
    w_value,
    w_out,
    w_gate,
    w_up,
    w_down,
    gain_attn_in,
    gain_query,
    gain_key,
    gain_attn_out,
    gain_ffn_in,
    gain_ffn_out,
):
    micro_count = tokens.shape[0]
    count = lax.axis_size("fsdp")
    devices = count * lax.axis_size("dp")
    core = lax.axis_index("dp")
    device = lax.axis_index("fsdp") * lax.axis_size("dp") + core
    slots = jnp.arange(micro_count, dtype=jnp.int32) * devices + device
    lengths = jnp.sum(
        jnp.where(slot_of[None, :] == slots[:, None], seq_lengths[None, :], 0), axis=1
    )
    rows = w_query.shape[0]
    gains = (gain_attn_in, gain_query, gain_key, gain_attn_out, gain_ffn_in, gain_ffn_out)
    gain_rows = tuple(piece.shape[0] for piece in gains)

    first_group = jnp.concatenate(
        [half_of(w_query, core, 1), jnp.where(core == 0, w_key, w_value), pack_gains(gains, rows)], axis=1
    )
    second_group = jnp.concatenate(
        [
            half_of(w_out, core, 0).T,
            half_of(w_gate, core, 1),
            half_of(w_up, core, 1),
            half_of(w_down, core, 0).T,
        ],
        axis=1,
    )
    query_mine, rest = gather_rows(first_group, 512, sizes)
    query_theirs = swap(query_mine)
    keyval_mine = rest[:, :256]
    keyval_theirs = swap(keyval_mine)
    key_all = jnp.where(core == 0, keyval_mine, keyval_theirs)
    value_all = jnp.where(core == 0, keyval_theirs, keyval_mine)
    all_gains = tuple(
        rest[:, 256 + i].reshape(count, rows)[:, :size].reshape(-1) for i, size in enumerate(gain_rows)
    )
    left_mine, right_mine = gather_rows(second_group, 1792, sizes)
    left_theirs, right_theirs = swap(left_mine), swap(right_mine)
    second_mine = jnp.concatenate([left_mine, right_mine], axis=1)
    second_theirs = jnp.concatenate([left_theirs, right_theirs], axis=1)

    def joined(start, stop):
        return jnp.concatenate([second_mine[:, start:stop], second_theirs[:, start:stop]], axis=1)

    params = (
        jnp.concatenate([query_mine, query_theirs], axis=1),
        key_all,
        value_all,
        joined(0, 512).T,
        joined(512, 1536),
        joined(1536, 2560),
        joined(2560, 3584).T,
    ) + all_gains
    kept, outputs, input_grads, grads = [], [], [], []
    for index in range(micro_count):
        saved, output = forward_pass(params, tokens[index], lengths[index])
        outputs.append(output)
        input_grad, grad = backward_pass(params, saved, cotangent[index], lengths[index])
        input_grads.append(input_grad)
        grads.append(grad)
    grads = tuple(sum(pieces[1:], pieces[0]) for pieces in zip(*grads))

    def low(piece):
        return piece.astype(jnp.bfloat16)

    g_query, g_key, g_value, g_out, g_gate, g_up, g_down = (low(piece) for piece in grads[:7])
    g_out, g_down = g_out.T, g_down.T
    gain_block = low(pack_gain_grads(grads[7:], count, rows))
    left = reduce_rows(
        jnp.concatenate([g_gate[:, :1024], g_out[:, :512]], axis=1),
        jnp.concatenate([g_gate[:, 1024:], g_out[:, 512:]], axis=1),
        sizes,
        False,
    )
    right = reduce_rows(
        jnp.concatenate([g_up[:, :1024], g_down[:, :1024]], axis=1),
        jnp.concatenate([g_up[:, 1024:], g_down[:, 1024:]], axis=1),
        sizes,
        True,
    )
    query_part = reduce_rows(g_query[:, :512], g_query[:, 512:], sizes, False)
    key_part = reduce_rows(
        jnp.concatenate([jnp.where(core == 0, g_key, g_value), gain_block], axis=1),
        jnp.concatenate([jnp.where(core == 0, g_value, g_key), gain_block], axis=1),
        sizes,
        True,
    )
    mine = jnp.concatenate([left, right, query_part, key_part[:, :256]], axis=1)
    theirs = swap(mine)

    def shard(start, stop):
        return in_order(core, mine[:, start:stop], theirs[:, start:stop])

    keyval = shard(4096, 4352)
    gain_shards = tuple(key_part[:size, 256 + i] for i, size in enumerate(gain_rows))
    return (
        jnp.stack(outputs),
        jnp.stack(input_grads),
        shard(3584, 4096),
        keyval[:, :256],
        keyval[:, 256:],
        shard(1024, 1536).T,
        shard(0, 1024),
        shard(1536, 2560),
        shard(2560, 3584).T,
    ) + gain_shards


def solution(mesh):
    sizes = factors(mesh.shape["fsdp"])
    in_specs = (
        P(None, ("fsdp", "dp"), None),
        P(None, ("fsdp", "dp"), None),
        P(),
        P(),
        P("fsdp", None),
        P("fsdp", None),
        P("fsdp", None),
        P(None, "fsdp"),
        P("fsdp", None),
        P("fsdp", None),
        P(None, "fsdp"),
        P("fsdp"),
        P("fsdp"),
        P("fsdp"),
        P("fsdp"),
        P("fsdp"),
        P("fsdp"),
    )
    out_specs = (
        P(None, ("fsdp", "dp"), None),
        P(None, ("fsdp", "dp"), None),
        P("fsdp", None),
        P("fsdp", None),
        P("fsdp", None),
        P(None, "fsdp"),
        P("fsdp", None),
        P("fsdp", None),
        P(None, "fsdp"),
        P("fsdp"),
        P("fsdp"),
        P("fsdp"),
        P("fsdp"),
        P("fsdp"),
        P("fsdp"),
    )
    return jax.shard_map(functools.partial(local, sizes), mesh=mesh, in_specs=in_specs, out_specs=out_specs, check_vma=False)
```

```python
import functools

import jax
import jax.numpy as jnp
import numpy as np
from jax import lax
from jax.experimental import pallas as pl
from jax.experimental.pallas import tpu as pltpu
from jax.sharding import PartitionSpec as P

HEADS = 4
HD = 256
norm_eps = 1e-06
rope_base = 10000.0
ROWS = 256
LOG2E = 1.4426950408889634
f32 = jnp.float32
bf16 = jnp.bfloat16


def dot(left, right):
    return jnp.dot(left, right, preferred_element_type=f32)


def dot_right(left, right):
    return lax.dot_general(left, right, (((1,), (1,)), ((), ())), preferred_element_type=f32)


def dot_left(left, right):
    return lax.dot_general(left, right, (((0,), (0,)), ((), ())), preferred_element_type=f32)


def inverse_rms(value):
    return lax.rsqrt(jnp.mean(value * value, axis=-1, keepdims=True) + norm_eps)


def norm_back(value, gain, grad):
    scale = inverse_rms(value)
    unit = value * scale
    weighted = gain * grad
    inner = jnp.mean(unit * weighted, axis=-1, keepdims=True)
    return scale * (weighted - unit * inner), jnp.sum(unit * grad, axis=0, keepdims=True)


def rotate(value, cosine, sine):
    half = value.shape[-1] // 2
    first = value[:, :half]
    second = value[:, half:]
    return jnp.concatenate([first * cosine - second * sine, second * cosine + first * sine], axis=1)


def as_row(column):
    return jnp.transpose(jnp.broadcast_to(column, (column.shape[0], 128)))[:8]


def key_after_query(transposed):
    shape = (ROWS, ROWS)
    query = lax.broadcasted_iota(jnp.int32, shape, 1 if transposed else 0)
    key = lax.broadcasted_iota(jnp.int32, shape, 0 if transposed else 1)
    return key > query


def key_and_value(core, mine, theirs):
    half = HEADS * HD // 2
    left, right = mine[:, half : half + HD], theirs[:, half : half + HD]
    first = jnp.full(left.shape, core[0], jnp.int32) == 0
    return jnp.where(first, left, right), jnp.where(first, right, left)


def attention_forward_kernel(
    core, tok, mine, theirs, gain_in, gain_q, gain_k, cos, sin,
    a_out, qlin_out, qrot_out, klin_out, krot_out, v_out, mixed_mine, mixed_theirs, lse_out, k_all, v_all,
):
    block = pl.program_id(1)
    inputs = tok[0].astype(f32)
    normed = (inputs * inverse_rms(inputs) * gain_in[...]).astype(bf16)
    a_out[0] = normed
    cosine, sine = cos[...], sin[...]

    def prepared(linear, gain):
        return rotate(linear * inverse_rms(linear) * gain, cosine, sine).astype(bf16)

    here = pl.ds(pl.multiple_of(block * ROWS, ROWS), ROWS)
    wk, wv = key_and_value(core, mine, theirs)
    key_lin = dot(normed, wk)
    klin_out[0] = key_lin
    key_rot = prepared(key_lin, gain_k[...])
    krot_out[0] = key_rot
    k_all[here, :] = key_rot
    value = dot(normed, wv).astype(bf16)
    v_out[0] = value
    v_all[here, :] = value
    for half, weight in enumerate((mine, theirs)):
        linear = dot(normed, weight[:, : HEADS * HD // 2])
        for head in range(2):
            part = linear[:, head * HD : (head + 1) * HD]
            qlin_out[0, 2 * half + head] = part
            qrot_out[0, 2 * half + head] = prepared(part, gain_q[...])

    def attend(steps):
        queries = qrot_out[0].reshape(HEADS * ROWS, HD)
        after = key_after_query(False)[None]
        mass = jnp.zeros((HEADS * ROWS, 128), f32)
        mixed = jnp.zeros((HEADS * ROWS, HD), f32)
        for step in steps:
            keys = pl.ds(pl.multiple_of((block - step) * ROWS, ROWS), ROWS)
            expon = jnp.exp2(dot_right(queries, k_all[keys, :]) * (LOG2E * HD**-0.5))
            if step != 1:
                expon = expon.reshape(HEADS, ROWS, ROWS)
                keep = jnp.logical_not(after) if step == 0 else after
                expon = jnp.where(keep, expon, 0.0).reshape(HEADS * ROWS, ROWS)
            mass = mass + (expon[:, :128] + expon[:, 128:])
            mixed = mixed + dot(expon.astype(bf16), v_all[keys, :])
        sums = jnp.sum(mass, axis=-1, keepdims=True)
        mixed = (mixed * (1.0 / sums)).astype(bf16)
        for head in range(HEADS):
            mixed_out = (mixed_mine, mixed_theirs)[head // 2]
            columns = slice((head % 2) * HD, (head % 2 + 1) * HD)
            mixed_out[0, :, columns] = mixed[head * ROWS : (head + 1) * ROWS]
        lse_out[0, 0] = as_row(jnp.log(sums) * LOG2E)

    pl.when(block == 0)(lambda: attend((0,)))
    pl.when(block == 1)(lambda: attend((1, 0)))
    pl.when(block >= 2)(lambda: attend((2, 1, 0)))


def feed_forward_kernel(
    lengths, tok, cot, mixed_mine, mixed_theirs, wide_mine, wide_theirs, deep_mine, deep_theirs,
    gain_ao, gain_fi, gain_fo,
    act_out, gh_out, gm_out, dots_out, fin_out, gres_out, gatt_out,
    inner_mine, inner_theirs, grad_mine, grad_theirs, gains_out, left_s, right_s,
):
    micro, block = pl.program_id(0), pl.program_id(1)
    rows = tok.shape[1]
    inputs = tok[0].astype(f32)
    place = block * rows + lax.broadcasted_iota(jnp.int32, (rows, 1), 0)
    valid = (place < lengths[micro]).astype(f32)
    half_width = wide_mine.shape[1] // 2
    attended = dot_right(mixed_mine[0], deep_mine[:, half_width:]) + dot_right(
        mixed_theirs[0], deep_theirs[:, half_width:]
    )
    hidden = inputs + attended * inverse_rms(attended) * gain_ao[...]
    ffn_in = (hidden * inverse_rms(hidden) * gain_fi[...]).astype(bf16)
    fin_out[0] = ffn_in
    result = jnp.zeros(inputs.shape, f32)
    chunk = 512
    rate, cubic = 0.7978845608028654, 0.044715
    for half in range(2):
        wide = (wide_mine, wide_theirs)[half]
        deep = (deep_mine, deep_theirs)[half]
        inner_out = (inner_mine, inner_theirs)[half]
        for start in range(0, half_width, chunk):
            columns = slice(start, start + chunk)
            kept = slice(half * half_width + start, half * half_width + start + chunk)
            shifted_columns = slice(half_width + start, half_width + start + chunk)
            gate = dot(ffn_in, wide[:, columns])
            up = dot(ffn_in, wide[:, shifted_columns])
            square = gate * gate
            tanh = jnp.tanh(gate * (rate + (rate * cubic) * square))
            side = 0.5 + 0.5 * tanh
            gelu = gate * side
            slope = side + gelu * (1.0 - tanh) * (rate + (3.0 * rate * cubic) * square)
            inner = (gelu * up).astype(bf16)
            inner_out[0, :, columns] = inner
            left_s[:, kept] = (up * slope).astype(bf16)
            right_s[:, kept] = gelu.astype(bf16)
            result = result + dot_right(inner, deep[:, columns])
    act_out[0] = (valid * (hidden + result * inverse_rms(result) * gain_fo[...])).astype(bf16)
    upstream = valid * cot[0].astype(f32)
    grad_result, g_fo = norm_back(result, gain_fo[...], upstream)
    grad_result = grad_result.astype(bf16)
    gres_out[0] = grad_result
    grad_in = jnp.zeros(inputs.shape, f32)
    for half in range(2):
        wide = (wide_mine, wide_theirs)[half]
        deep = (deep_mine, deep_theirs)[half]
        grad_out = (grad_mine, grad_theirs)[half]
        for start in range(0, half_width, chunk):
            columns = slice(start, start + chunk)
            kept = slice(half * half_width + start, half * half_width + start + chunk)
            shifted_columns = slice(half_width + start, half_width + start + chunk)
            grad_inner = dot(grad_result, deep[:, columns])
            grad_gate = (grad_inner * left_s[:, kept].astype(f32)).astype(bf16)
            grad_up = (grad_inner * right_s[:, kept].astype(f32)).astype(bf16)
            grad_out[0, :, columns] = grad_gate
            grad_out[0, :, shifted_columns] = grad_up
            grad_in = grad_in + dot_right(grad_gate, wide[:, columns])
            grad_in = grad_in + dot_right(grad_up, wide[:, shifted_columns])
    grad_hidden, g_fi = norm_back(hidden, gain_fi[...], grad_in)
    grad_hidden = upstream + grad_hidden
    gh_out[0] = grad_hidden
    grad_att, g_ao = norm_back(attended, gain_ao[...], grad_hidden)
    grad_att = grad_att.astype(bf16)
    gatt_out[0] = grad_att
    for head in range(HEADS):
        weight, mixed = ((deep_mine, mixed_mine), (deep_theirs, mixed_theirs))[head // 2]
        columns = slice((head % 2) * HD, (head % 2 + 1) * HD)
        out_columns = slice(half_width + columns.start, half_width + columns.stop)
        grad_mixed = dot(grad_att, weight[:, out_columns]).astype(bf16)
        gm_out[0, head] = grad_mixed
        product = jnp.sum(grad_mixed.astype(f32) * mixed[0, :, columns].astype(f32), axis=-1, keepdims=True)
        dots_out[0, 0, :, head * rows : (head + 1) * rows] = as_row(product)

    @pl.when((micro == 0) & (block == 0))
    def _():
        gains_out[...] = jnp.zeros(gains_out.shape, f32)

    gains_out[0:1, :] += g_ao
    gains_out[1:2, :] += g_fi
    gains_out[2:3, :] += g_fo


def attention_backward_kernel(
    qrot, qlin, gm, lse, dots, cos, sin, krot, val, klin, cos_late, sin_late, tok, gh,
    core, mine, theirs, gain_in, gain_q, gain_k,
    input_out, grad_mine, grad_theirs, gains_out, dk, dv, gq_all,
):
    micro, step = pl.program_id(0), pl.program_id(1)

    @pl.when((micro == 0) & (step == 0))
    def _():
        gains_out[...] = jnp.zeros(gains_out.shape, f32)

    def unrotated(grad, cosine, sine):
        return rotate(grad * HD**-0.5, cosine, -sine)

    def attend(backs):
        queries = qrot[0].reshape(HEADS * ROWS, HD)
        grads = gm[0].reshape(HEADS * ROWS, HD)
        after = key_after_query(True)
        after = jnp.concatenate([after] * HEADS, axis=1)
        log_mass, row_dot = lse[0, 0, 0:1], dots[0, 0, 0:1]
        grad_queries = jnp.zeros((HEADS * ROWS, HD), f32)
        for back in backs:
            keys = pl.ds(pl.multiple_of((step - back) * ROWS, ROWS), ROWS)
            key, value = krot[0, keys, :], val[0, keys, :]
            probs = jnp.exp2(dot_right(key, queries) * (LOG2E * HD**-0.5) - log_mass)
            if back != 1:
                probs = jnp.where(jnp.logical_not(after) if back == 0 else after, probs, 0.0)
            grad_probs = dot_right(value, grads)
            grad_scores = (probs * (grad_probs - row_dot)).astype(bf16)
            grad_value = dot(probs.astype(bf16), grads)
            grad_key = dot(grad_scores, queries)
            if back == 0:
                dv[keys, :] = grad_value
                dk[keys, :] = grad_key
            else:
                dv[keys, :] += grad_value
                dk[keys, :] += grad_key
            grad_queries = grad_queries + dot_left(grad_scores, key)
        here = pl.ds(pl.multiple_of(step * ROWS, ROWS), ROWS)
        for head in range(HEADS):
            turned = unrotated(grad_queries[head * ROWS : (head + 1) * ROWS], cos[...], sin[...])
            grad_lin, g_q = norm_back(qlin[0, head], gain_q[...], turned)
            gq_all[here, head * HD : (head + 1) * HD] = grad_lin.astype(bf16)
            gains_out[1:2, :HD] += g_q

    pl.when(step == 0)(lambda: attend((0,)))
    pl.when(step == 1)(lambda: attend((1, 0)))
    pl.when((step == 2) | (step == 3))(lambda: attend((2, 1, 0)))

    @pl.when(step >= 2)
    def _():
        here = pl.ds(pl.multiple_of((step - 2) * ROWS, ROWS), ROWS)
        turned = unrotated(dk[here, :], cos_late[...], sin_late[...])
        grad_key, g_k = norm_back(klin[0], gain_k[...], turned)
        grad_key = grad_key.astype(bf16)
        grad_value = dv[here, :].astype(bf16)
        half = HEADS * HD // 2
        first, second = gq_all[here, :half], gq_all[here, half:]
        grad_mine[0, :, :half] = first
        grad_theirs[0, :, :half] = second
        is_first = jnp.full(grad_key.shape, core[0], jnp.int32) == 0
        grad_mine[0, :, half:] = jnp.where(is_first, grad_key, grad_value)
        grad_theirs[0, :, half:] = jnp.where(is_first, grad_value, grad_key)
        wk, wv = key_and_value(core, mine, theirs)
        grad_in = (
            dot_right(first, mine[:, :half])
            + dot_right(second, theirs[:, :half])
            + dot_right(grad_key, wk)
            + dot_right(grad_value, wv)
        )
        grad_inputs, g_in = norm_back(tok[0].astype(f32), gain_in[...], grad_in)
        input_out[0] = (gh[0] + grad_inputs).astype(bf16)
        gains_out[0:1, :] += g_in
        gains_out[2:3, :HD] += g_k


def whole(array):
    return pl.BlockSpec(array.shape, lambda m, i: (0,) * array.ndim, pipeline_mode=pl.Buffered(1))


def struct(shape, dtype):
    return jax.ShapeDtypeStruct(shape, dtype)


def params(limit):
    return pltpu.CompilerParams(vmem_limit_bytes=limit << 20, dimension_semantics=("arbitrary", "arbitrary"))


def cost(flops, size):
    return pl.CostEstimate(flops=flops, bytes_accessed=size, transcendentals=0)


def rows_spec(width, place=lambda i: i, micro=0):
    return pl.BlockSpec((1, ROWS, width), lambda m, i: (m + micro, place(i), 0))


def heads_spec(place=lambda i: i, micro=0):
    return pl.BlockSpec((1, HEADS, ROWS, HD), lambda m, i: (m + micro, 0, place(i), 0))


def stat_spec(place=lambda i: i, micro=0):
    return pl.BlockSpec((1, 1, 8, HEADS * ROWS), lambda m, i: (m + micro, place(i), 0, 0))


def onward(kernel, inputs, earlier):
    return lambda *refs: kernel(*refs[:inputs], *refs[inputs + earlier :])


def table_spec(place=lambda i: i):
    return pl.BlockSpec((ROWS, HD // 2), lambda m, i: (place(i), 0))


def rope_tables(rows, head_dim):
    half = head_dim // 2
    inverse = 1.0 / rope_base ** (np.arange(half, dtype=np.float32) * np.float32(2.0 / head_dim))
    angle = np.arange(rows, dtype=np.float32)[:, None] * inverse.astype(np.float32)[None, :]
    return jnp.asarray(np.cos(angle), f32), jnp.asarray(np.sin(angle), f32)


def attention_forward(core, tokens, weights, gains, tables, micro, earlier=()):
    micros, rows, width = tokens.shape
    blocks = rows // ROWS
    half = HEADS * HD // 2
    shapes = (
        struct((micros, rows, width), bf16),
        struct((micros, HEADS, rows, HD), f32),
        struct((micros, HEADS, rows, HD), bf16),
        struct((micros, rows, HD), f32),
        struct((micros, rows, HD), bf16),
        struct((micros, rows, HD), bf16),
        struct((micros, rows, half), bf16),
        struct((micros, rows, half), bf16),
        struct((micros, blocks, 8, HEADS * ROWS), f32),
    )
    heads = heads_spec(micro=micro)
    narrow = rows_spec(HD, micro=micro)
    specs = (rows_spec(width, micro=micro), heads, heads, narrow, narrow, narrow) + (
        rows_spec(half, micro=micro),
        rows_spec(half, micro=micro),
        stat_spec(micro=micro),
    )
    operands = (core, tokens, *weights, *gains, *tables)
    return pl.pallas_call(
        onward(attention_forward_kernel, len(operands), len(earlier)),
        grid=(1, blocks),
        in_specs=[pl.BlockSpec(memory_space=pltpu.SMEM), rows_spec(width, micro=micro)] + [whole(w) for w in weights] + [whole(g) for g in gains]
        + [table_spec()] * 2 + [pl.BlockSpec(memory_space=pl.ANY)] * len(earlier),
        out_specs=specs,
        out_shape=shapes,
        scratch_shapes=[pltpu.VMEM((rows, HD), bf16), pltpu.VMEM((rows, HD), bf16)],
        input_output_aliases={len(operands) + i: i for i in range(len(earlier))},
        compiler_params=params(48),
        cost_estimate=cost(5 * 10**9, 20 << 20),
        name="attention_forward",
    )(*operands, *earlier)


def feed_forward(lengths, tokens, cotangent, mixed, weights, gains):
    micros, rows, width = tokens.shape
    blocks = rows // ROWS
    hidden = weights[0].shape[1] // 2
    shapes = (
        struct((micros, rows, width), bf16),
        struct((micros, rows, width), f32),
        struct((micros, HEADS, rows, HD), bf16),
        struct((micros, blocks, 8, HEADS * ROWS), f32),
        struct((micros, rows, width), bf16),
        struct((micros, rows, width), bf16),
        struct((micros, rows, width), bf16),
    ) + (struct((micros, rows, hidden), bf16),) * 2 + (struct((micros, rows, 2 * hidden), bf16),) * 2 + (
        struct((8, width), f32),
    )
    specs = (
        rows_spec(width), rows_spec(width), heads_spec(), stat_spec(), rows_spec(width), rows_spec(width), rows_spec(width),
    ) + (rows_spec(hidden),) * 2 + (rows_spec(2 * hidden),) * 2 + (
        pl.BlockSpec((8, width), lambda m, i: (0, 0)),
    )
    return pl.pallas_call(
        feed_forward_kernel,
        grid=(micros, blocks),
        in_specs=[pl.BlockSpec(memory_space=pltpu.SMEM), rows_spec(width), rows_spec(width)]
        + [rows_spec(HEADS * HD // 2)] * 2
        + [whole(w) for w in weights]
        + [whole(g) for g in gains],
        out_specs=specs,
        out_shape=shapes,
        scratch_shapes=[pltpu.VMEM((ROWS, 2 * hidden), bf16), pltpu.VMEM((ROWS, 2 * hidden), bf16)],
        compiler_params=params(56),
        cost_estimate=cost(38 * 10**9, 80 << 20),
        name="feed_forward",
    )(lengths, tokens, cotangent, *mixed, *weights, *gains)


def attention_backward(core, saved, grads, tokens, weights, gains, tables, micro, earlier=()):
    _, qlin, qrot, klin, krot, value, _, _, lse = saved
    grad_hidden, grad_mixed, dots = grads
    micros, rows, width = tokens.shape
    blocks = rows // ROWS
    half = HEADS * HD // 2

    def early(i):
        return jnp.minimum(i, blocks - 1)

    def late(i):
        return jnp.maximum(i - 2, 0)

    keys = pl.BlockSpec((1, rows, HD), lambda m, i: (m + micro, 0, 0))
    shapes = (
        struct((micros, rows, width), bf16),
        struct((micros, rows, half + HD), bf16),
        struct((micros, rows, half + HD), bf16),
        struct((8, width), f32),
    )
    specs = tuple(rows_spec(size, late, micro) for size in (width, half + HD, half + HD)) + (
        pl.BlockSpec((8, width), lambda m, i: (0, 0)),
    )
    operands = (
        qrot, qlin, grad_mixed, lse, dots, *tables, krot, value, klin, *tables, tokens, grad_hidden, core, *weights, *gains,
    )
    return pl.pallas_call(
        onward(attention_backward_kernel, len(operands), len(earlier)),
        grid=(1, blocks + 2),
        in_specs=[heads_spec(early, micro)] * 3 + [stat_spec(early, micro)] * 2 + [table_spec(early)] * 2 + [keys] * 2
        + [rows_spec(HD, late, micro)] + [table_spec(late)] * 2 + [rows_spec(width, late, micro)] * 2
        + [pl.BlockSpec(memory_space=pltpu.SMEM)] + [whole(w) for w in weights] + [whole(g) for g in gains]
        + [pl.BlockSpec(memory_space=pl.ANY)] * len(earlier),
        out_specs=specs,
        out_shape=shapes,
        scratch_shapes=[pltpu.VMEM((rows, HD), f32), pltpu.VMEM((rows, HD), f32), pltpu.VMEM((rows, HEADS * HD), bf16)],
        input_output_aliases={len(operands) + i: i for i in range(len(earlier))},
        compiler_params=params(48),
        cost_estimate=cost(9 * 10**9, 20 << 20),
        name="attention_backward",
    )(*operands, *earlier)


def weight_grad(left, right):
    return dot_left(left.reshape(-1, left.shape[-1]), right.reshape(-1, right.shape[-1])).astype(bf16)


def fold(operands, groups, scalars, grid, outs):
    flat_terms = [term for group in groups for columns in group for term in columns]

    def kernel(_, *refs):
        sources, targets = refs[: len(flat_terms)], refs[len(flat_terms) :]
        at = 0
        for group, target in zip(groups, targets):
            start = 0
            for columns in group:
                value = sources[at][...].astype(f32)
                for more in range(1, len(columns)):
                    value = value + sources[at + more][...].astype(f32)
                width = value.shape[-1]
                target[..., start : start + width] = value.reshape(target.shape[:-1] + (width,)).astype(target.dtype)
                start += width
                at += len(columns)

    return pl.pallas_call(
        kernel,
        grid_spec=pltpu.PrefetchScalarGridSpec(
            num_scalar_prefetch=1,
            grid=grid,
            in_specs=[pl.BlockSpec(block, index) for _, block, index in flat_terms],
            out_specs=tuple(pl.BlockSpec(block, index) for _, block, index, _ in outs),
        ),
        out_shape=tuple(struct(shape, kind) for shape, _, _, kind in outs),
        compiler_params=pltpu.CompilerParams(vmem_limit_bytes=48 << 20, dimension_semantics=("arbitrary",)),
        cost_estimate=cost(10**6, 8 << 20),
        name="fold",
    )(scalars, *[operands[i] for i, _, _ in flat_terms])


def factors(count):
    side = 1
    while 2 * side**3 < count:
        side += 1
    return (2 * side, side, side) if 2 * side**3 == count else (count, 1, 1)


def place(sizes, axis):
    index = lax.axis_index("fsdp")
    for size in sizes[axis + 1 :]:
        index = index // size
    return index % sizes[axis]


def shifted(sizes, axis, step):
    stride = 1
    for size in sizes[axis + 1 :]:
        stride *= size
    pairs = []
    for index in range(sizes[0] * sizes[1] * sizes[2]):
        at = (index // stride) % sizes[axis]
        pairs.append((index, index + ((at + step) % sizes[axis] - at) * stride))
    return pairs


def tie(*trees):
    return lax.optimization_barrier(trees)


def ring_pairs(sizes, turn, step):
    pairs = []
    for core in range(2):
        axis = 1 if (core == 0) == (turn == 0) else 2
        pairs += [(2 * source + core, 2 * target + core) for source, target in shifted(sizes, axis, step)]
    return pairs


def place_at(sizes, turn, core):
    first, second = place(sizes, 1), place(sizes, 2)
    return jnp.where(core == 0, first, second) if turn == 0 else jnp.where(core == 0, second, first)


def sent_turn(block, sizes, turn):
    return [block] + [
        lax.ppermute(block, ("fsdp", "dp"), ring_pairs(sizes, turn, step)) for step in range(1, sizes[1])
    ]


def sent_z(block, sizes):
    return [block] + [lax.ppermute(block, "fsdp", shifted(sizes, 0, step)) for step in range(1, sizes[0])]


def joined_z(pieces, sizes):
    here, size = place(sizes, 0), sizes[0]
    rows = []
    for at in range(size):
        row = pieces[-1]
        for step in range(size - 1):
            row = jnp.where((here - at) % size == step, pieces[step], row)
        rows.append(row)
    return jnp.stack(rows)


def sent_middle(block, sizes, core):
    return sent_turn(block, sizes, 0)


def joined_middle(pieces, sizes, core):
    here, side = place_at(sizes, 0, core), sizes[1]
    if side == 1:
        return pieces[0][:, None]
    if side == 2:
        own, other = pieces
        return jnp.stack([jnp.where(here == 0, own, other), jnp.where(here == 0, other, own)], axis=1)
    out = jnp.zeros(pieces[0].shape[:1] + (side,) + pieces[0].shape[1:], pieces[0].dtype)
    for step, piece in enumerate(pieces):
        out = lax.dynamic_update_slice_in_dim(out, piece[:, None], (here - step) % side, 1)
    return out


def sent_last(block, sizes, core):
    return sent_turn(block, sizes, 1)


def joined_last(pieces, sizes, core):
    here, side = place_at(sizes, 1, core), sizes[1]
    if side == 2:
        own, other = pieces
        low = jnp.where(here == 0, own, other)
        high = jnp.where(here == 0, other, own)
        cross = [jnp.where(core == 0, high[:, 0], low[:, 1]), jnp.where(core == 0, low[:, 1], high[:, 0])]
        return jnp.stack([low[:, 0], cross[0], cross[1], high[:, 1]], axis=1)
    out = jnp.zeros(pieces[0].shape[:1] + (side * side,) + pieces[0].shape[2:], pieces[0].dtype)
    for step, piece in enumerate(pieces):
        there = (here - step) % side
        for k in range(side):
            at = jnp.where(core == 0, side * k + there, side * there + k)
            out = lax.dynamic_update_slice_in_dim(out, piece[:, k : k + 1], at, 1)
    return out


def gather_middle(block, sizes, core):
    return joined_middle(sent_middle(block, sizes, core), sizes, core)


def gather_last(block, sizes, core):
    return joined_last(sent_last(block, sizes, core), sizes, core)


def flat(block):
    return block.reshape(-1, block.shape[-1])


def swap(block):
    return lax.ppermute(block, "dp", [(0, 1), (1, 0)])


def total(parts):
    out = parts[0].astype(jnp.float32)
    for part in parts[1:]:
        out = out + part.astype(jnp.float32)
    return out


def boxed(mine, arrived, sizes):
    box = (sizes[0], sizes[1] * sizes[2], mine.shape[0] // (sizes[0] * sizes[1] * sizes[2]), mine.shape[1])
    return [mine.reshape(box), arrived.reshape(box)]


def moved(sent, sizes, turn):
    return [
        lax.ppermute(piece, ("fsdp", "dp"), ring_pairs(sizes, turn, step)) for step, piece in enumerate(sent, 1)
    ]


def moved_z(sent, sizes):
    return [lax.ppermute(piece, "fsdp", shifted(sizes, 0, step)) for step, piece in enumerate(sent, 1)]


def fold_first(bundle, sizes, core):
    here, side = place_at(sizes, 1, core), sizes[1]
    places = []
    for step in range(side):
        there = (here + step) % side
        places += [jnp.where(core == 0, side * k + there, side * there + k) for k in range(side)]
    box = bundle[0][0].shape
    width = sum(parts[0].shape[-1] for parts in bundle)
    operands, groups, outs = [], [], []
    for step in range(side):
        group = []
        for parts in bundle:
            block = (box[0], 1, box[2], parts[0].shape[-1])
            columns = []
            for part in parts:
                operands.append(part)
                columns.append((len(operands) - 1, block, lambda k, at, step=step: (0, at[step * side + k], 0, 0)))
            group.append(columns)
        groups.append(group)
        outs.append(
            (
                (box[0], side, box[2], width),
                (box[0], 1, box[2], width),
                lambda k, at: (0, k, 0, 0),
                bf16 if step else f32,
            )
        )
    keep, *sent = fold(operands, groups, jnp.stack(places).astype(jnp.int32), (side,), outs)
    return keep, sent


def fold_middle(bundle, sizes, core):
    here, side = place_at(sizes, 0, core), sizes[1]
    box = bundle[0][0].shape
    width = sum(parts[0].shape[-1] for parts in bundle)
    operands, groups, outs = [], [], []
    for step in range(side):
        group = []
        for parts in bundle:
            block = (1, 1, box[2], parts[0].shape[-1])
            columns = []
            for part in parts:
                operands.append(part)
                columns.append((len(operands) - 1, block, lambda z, at, step=step: (z, at[step], 0, 0)))
            group.append(columns)
        groups.append(group)
        outs.append(
            ((box[0], box[2], width), (1, box[2], width), lambda z, at: (z, 0, 0), bf16 if step else f32)
        )
    places = jnp.stack([(here + step) % side for step in range(side)]).astype(jnp.int32)
    keep, *sent = fold(operands, groups, places, (box[0],), outs)
    return keep, sent


def fold_z(parts, sizes):
    here, size = place(sizes, 0), sizes[0]
    _, rows, width = parts[0].shape
    groups, outs = [], []
    for step in range(size):
        groups.append(
            [[(i, (1, rows, width), lambda z, at, step=step: (at[step], 0, 0)) for i in range(len(parts))]]
        )
        outs.append(((rows, width), (rows, width), lambda z, at: (0, 0), bf16 if step else f32))
    places = jnp.stack([(here + step) % size for step in range(size)]).astype(jnp.int32)
    keep, *sent = fold(parts, groups, places, (1,), outs)
    return keep, sent


def half_of(array, core, axis):
    size = array.shape[axis] // 2
    return lax.dynamic_slice_in_dim(array, core * size, size, axis)


def in_order(core, mine, theirs):
    return jnp.concatenate([jnp.where(core == 0, mine, theirs), jnp.where(core == 0, theirs, mine)], axis=1)


def pack_gains(pieces, rows):
    columns = [jnp.pad(piece, (0, rows - piece.shape[0])) for piece in pieces]
    return jnp.pad(jnp.stack(columns, axis=1), ((0, 0), (0, 128 - len(columns))))


def pack_gain_grads(pieces, count, rows):
    columns = [
        jnp.pad(piece.reshape(count, -1), ((0, 0), (0, rows - piece.shape[0] // count))).reshape(-1)
        for piece in pieces
    ]
    return jnp.pad(jnp.stack(columns, axis=1), ((0, 0), (0, 128 - len(columns))))


def local(
    sizes,
    tokens,
    cotangent,
    seq_lengths,
    slot_of,
    w_query,
    w_key,
    w_value,
    w_out,
    w_gate,
    w_up,
    w_down,
    gain_attn_in,
    gain_query,
    gain_key,
    gain_attn_out,
    gain_ffn_in,
    gain_ffn_out,
):
    micro_count = tokens.shape[0]
    count = lax.axis_size("fsdp")
    devices = count * lax.axis_size("dp")
    core = lax.axis_index("dp")
    device = lax.axis_index("fsdp") * lax.axis_size("dp") + core
    slots = jnp.arange(micro_count, dtype=jnp.int32) * devices + device
    lengths = jnp.sum(
        jnp.where(slot_of[None, :] == slots[:, None], seq_lengths[None, :], 0), axis=1
    )
    rows = w_query.shape[0]
    gains = (gain_attn_in, gain_query, gain_key, gain_attn_out, gain_ffn_in, gain_ffn_out)
    gain_rows = tuple(piece.shape[0] for piece in gains)

    half, hidden = HEADS * HD // 2, w_gate.shape[1] // 2
    first = jnp.concatenate(
        [half_of(w_query, core, 1), jnp.where(core == 0, w_key, w_value), pack_gains(gains, rows)], axis=1
    )
    wide = jnp.concatenate([half_of(w_gate, core, 1), half_of(w_up, core, 1)], axis=1)
    deep = jnp.concatenate([half_of(w_down, core, 0).T, half_of(w_out, core, 0).T], axis=1)
    first = sent_z(first, sizes)
    first, wide = tie(first, wide)
    wide = sent_z(wide, sizes)
    first = sent_middle(joined_z(first, sizes), sizes, core)
    first, wide, deep = tie(first, wide, deep)
    first = sent_last(joined_middle(first, sizes, core), sizes, core)
    first, wide = tie(first, wide)
    wide = sent_middle(joined_z(wide, sizes), sizes, core)
    deep = sent_z(deep, sizes)
    first = flat(joined_last(first, sizes, core))
    attn_weights = (first, swap(first))
    full_gains = [
        first[:, half + HD + i].reshape(count, rows)[:, :size].reshape(1, -1).astype(f32)
        for i, size in enumerate(gain_rows)
    ]
    tables = rope_tables(tokens.shape[1], HD)
    which = jnp.reshape(core, (1,)).astype(jnp.int32)
    wide, deep, attn_weights = tie(wide, deep, attn_weights)
    wide, deep = joined_middle(wide, sizes, core), joined_z(deep, sizes)
    wide, deep, attn_weights = tie(wide, deep, attn_weights)
    wide, deep = sent_last(wide, sizes, core), sent_middle(deep, sizes, core)
    saved = attention_forward(which, tokens, attn_weights, full_gains[:3], tables, 0)
    wide, deep, saved = tie(wide, deep, saved)
    wide = flat(joined_last(wide, sizes, core))
    deep = joined_middle(deep, sizes, core)
    wide, deep, saved = tie(wide, deep, saved)
    deep = sent_last(deep, sizes, core)
    for micro in range(1, micro_count):
        saved = attention_forward(which, tokens, attn_weights, full_gains[:3], tables, micro, saved)
    deep, saved = tie(deep, saved)
    wide_swapped = swap(wide)
    deep = flat(joined_last(deep, sizes, core))
    ffn_weights = (wide, wide_swapped, deep, swap(deep))

    mixed = saved[6:8]
    (
        outputs, grad_hidden, grad_mixed, dots, ffn_in, grad_result, grad_att,
        inner_mine, inner_theirs, grad_mine, grad_theirs, gains_ffn,
    ) = feed_forward(lengths, tokens, cotangent, mixed, ffn_weights, full_gains[3:])
    wide = weight_grad(ffn_in, grad_theirs)
    wide, grad_mine = tie(wide, grad_mine)
    wide_arrived = swap(wide)
    wide = weight_grad(ffn_in, grad_mine)
    wide, inner_theirs, grad_att = tie(wide, inner_theirs, grad_att)
    deep = [weight_grad(grad_result, inner_theirs), weight_grad(grad_att, mixed[1])]
    wide_keep, wide_sent = fold_first([boxed(wide, wide_arrived, sizes)], sizes, core)
    deep, wide_sent, inner_mine, grad_att = tie(deep, wide_sent, inner_mine, grad_att)
    wide_arrived = moved(wide_sent, sizes, 1)
    deep_arrived = [swap(piece) for piece in deep]
    deep = [weight_grad(grad_result, inner_mine), weight_grad(grad_att, mixed[0])]
    deep = [boxed(own, piece, sizes) for own, piece in zip(deep, deep_arrived)]
    deep_keep, deep_sent = fold_first(deep, sizes, core)
    deep_sent, wide_arrived = tie(deep_sent, wide_arrived)
    wide_keep, wide_sent = fold_middle([[wide_keep, *wide_arrived]], sizes, core)
    wide_sent, deep_sent, grad_mixed = tie(wide_sent, deep_sent, grad_mixed)
    wide_arrived, deep_arrived = moved(wide_sent, sizes, 0), moved(deep_sent, sizes, 1)
    for micro in range(micro_count):
        *back, gains_own = attention_backward(
            which, saved, (grad_hidden, grad_mixed, dots), tokens, attn_weights, full_gains[:3], tables,
            micro, back if micro else (),
        )
        gains_attn = gains_attn + gains_own if micro else gains_own
        if micro == 0:
            wide_arrived, deep_arrived, back = tie(wide_arrived, deep_arrived, back)
            wide_keep, wide_sent = fold_z([wide_keep, *wide_arrived], sizes)
            deep_keep, deep_sent = fold_middle([[deep_keep, *deep_arrived]], sizes, core)
            wide_sent, deep_sent, back = tie(wide_sent, deep_sent, back)
            deep_arrived, wide_arrived = moved(deep_sent, sizes, 0), moved_z(wide_sent, sizes)
    deep_arrived, wide_arrived, back = tie(deep_arrived, wide_arrived, back)
    deep_keep, deep_sent = fold_z([deep_keep, *deep_arrived], sizes)
    deep_sent, back = tie(deep_sent, back)
    deep_arrived = moved_z(deep_sent, sizes)
    input_grad, grad_mine, grad_theirs = back
    gain_grads = (
        gains_attn[0], gains_attn[1, :HD], gains_attn[2, :HD], gains_ffn[0], gains_ffn[1], gains_ffn[2],
    )
    gain_block = pack_gain_grads(gain_grads, count, rows).astype(bf16)
    normed = saved[0]
    d_theirs = weight_grad(normed, grad_theirs)
    d_theirs, grad_mine = tie(d_theirs, grad_mine)
    d_mine = weight_grad(normed, grad_mine)
    deep_arrived, d_mine = tie(deep_arrived, d_mine)
    narrow = [boxed(d_mine, swap(d_theirs), sizes), boxed(gain_block, swap(gain_block), sizes)]
    narrow_keep, narrow_sent = fold_first(narrow, sizes, core)
    narrow_arrived = moved(narrow_sent, sizes, 1)
    wide = total([wide_keep, *wide_arrived])
    deep = total([deep_keep, *deep_arrived])
    narrow_arrived, wide, deep = tie(narrow_arrived, wide, deep)
    narrow_keep, narrow_sent = fold_middle([[narrow_keep, *narrow_arrived]], sizes, core)
    narrow_arrived = moved(narrow_sent, sizes, 0)
    narrow_keep, narrow_sent = fold_z([narrow_keep, *narrow_arrived], sizes)
    narrow = total([narrow_keep, *moved_z(narrow_sent, sizes)])
    mine = jnp.concatenate([wide, deep, narrow[:, : half + HD]], axis=1)
    theirs = swap(mine)

    def shard(start, width):
        return in_order(core, mine[:, start : start + width], theirs[:, start : start + width])

    query_at = 3 * hidden + half
    keyval = shard(query_at + half, HD)
    gain_shards = tuple(narrow[:size, half + HD + i] for i, size in enumerate(gain_rows))
    return (
        outputs,
        input_grad,
        shard(query_at, half),
        keyval[:, :HD],
        keyval[:, HD:],
        shard(3 * hidden, half).T,
        shard(0, hidden),
        shard(hidden, hidden),
        shard(2 * hidden, hidden).T,
    ) + gain_shards


def solution(mesh):
    sizes = factors(mesh.shape["fsdp"])
    in_specs = (
        P(None, ("fsdp", "dp"), None),
        P(None, ("fsdp", "dp"), None),
        P(),
        P(),
        P("fsdp", None),
        P("fsdp", None),
        P("fsdp", None),
        P(None, "fsdp"),
        P("fsdp", None),
        P("fsdp", None),
        P(None, "fsdp"),
        P("fsdp"),
        P("fsdp"),
        P("fsdp"),
        P("fsdp"),
        P("fsdp"),
        P("fsdp"),
    )
    out_specs = (
        P(None, ("fsdp", "dp"), None),
        P(None, ("fsdp", "dp"), None),
        P("fsdp", None),
        P("fsdp", None),
        P("fsdp", None),
        P(None, "fsdp"),
        P("fsdp", None),
        P("fsdp", None),
        P(None, "fsdp"),
        P("fsdp"),
        P("fsdp"),
        P("fsdp"),
        P("fsdp"),
        P("fsdp"),
        P("fsdp"),
    )
    return jax.shard_map(functools.partial(local, sizes), mesh=mesh, in_specs=in_specs, out_specs=out_specs, check_vma=False)
```

```python
import functools

import jax
import jax.numpy as jnp
import numpy as np
from jax import lax
from jax.experimental import pallas as pl
from jax.experimental.pallas import tpu as pltpu
from jax.sharding import PartitionSpec as P

HEADS = 4
HD = 256
norm_eps = 1e-06
rope_base = 10000.0
ROWS = 256
FFN_ROWS = 512
CHUNK = 512
LOG2E = 1.4426950408889634
f32 = jnp.float32
bf16 = jnp.bfloat16


def dot(left, right):
    return jnp.dot(left, right, preferred_element_type=f32)


def dot_right(left, right):
    return lax.dot_general(left, right, (((1,), (1,)), ((), ())), preferred_element_type=f32)


def dot_left(left, right):
    return lax.dot_general(left, right, (((0,), (0,)), ((), ())), preferred_element_type=f32)


def inverse_rms(value):
    return lax.rsqrt(jnp.mean(value * value, axis=-1, keepdims=True) + norm_eps)


def norm_back(value, gain, grad):
    scale = inverse_rms(value)
    unit = value * scale
    weighted = gain * grad
    inner = jnp.mean(unit * weighted, axis=-1, keepdims=True)
    return scale * (weighted - unit * inner), jnp.sum(unit * grad, axis=0, keepdims=True)


def rotate(value, cosine, sine):
    half = value.shape[-1] // 2
    first = value[:, :half]
    second = value[:, half:]
    return jnp.concatenate([first * cosine - second * sine, second * cosine + first * sine], axis=1)


def as_row(column):
    return jnp.transpose(jnp.broadcast_to(column, (column.shape[0], 128)))[:8]


def key_after_query(transposed):
    shape = (ROWS, ROWS)
    query = lax.broadcasted_iota(jnp.int32, shape, 1 if transposed else 0)
    key = lax.broadcasted_iota(jnp.int32, shape, 0 if transposed else 1)
    return key > query


def key_and_value(core, mine, theirs):
    half = HEADS * HD // 2
    left, right = mine[:, half : half + HD], theirs[:, half : half + HD]
    first = jnp.full(left.shape, core[0], jnp.int32) == 0
    return jnp.where(first, left, right), jnp.where(first, right, left)


def attention_forward_kernel(
    core, tok, mine, theirs, gain_in, gain_q, gain_k, cos, sin,
    a_out, qlin_out, qrot_out, klin_out, krot_out, v_out, mixed_mine, mixed_theirs, lse_out, k_all, v_all,
):
    block = pl.program_id(1)
    inputs = tok[0].astype(f32)
    normed = (inputs * inverse_rms(inputs) * gain_in[...]).astype(bf16)
    a_out[0] = normed
    cosine, sine = cos[...], sin[...]

    def prepared(linear, gain):
        return rotate(linear * inverse_rms(linear) * gain, cosine, sine).astype(bf16)

    here = pl.ds(pl.multiple_of(block * ROWS, ROWS), ROWS)
    wk, wv = key_and_value(core, mine, theirs)
    key_lin = dot(normed, wk)
    klin_out[0] = key_lin
    key_rot = prepared(key_lin, gain_k[...])
    krot_out[0] = key_rot
    k_all[here, :] = key_rot
    value = dot(normed, wv).astype(bf16)
    v_out[0] = value
    v_all[here, :] = value
    for half, weight in enumerate((mine, theirs)):
        linear = dot(normed, weight[:, : HEADS * HD // 2])
        for head in range(2):
            part = linear[:, head * HD : (head + 1) * HD]
            qlin_out[0, 2 * half + head] = part
            qrot_out[0, 2 * half + head] = prepared(part, gain_q[...])

    def attend(steps):
        queries = qrot_out[0].reshape(HEADS * ROWS, HD)
        after = key_after_query(False)[None]
        mass = jnp.zeros((HEADS * ROWS, 128), f32)
        mixed = jnp.zeros((HEADS * ROWS, HD), f32)
        for step in steps:
            keys = pl.ds(pl.multiple_of((block - step) * ROWS, ROWS), ROWS)
            expon = jnp.exp2(dot_right(queries, k_all[keys, :]) * (LOG2E * HD**-0.5))
            if step != 1:
                expon = expon.reshape(HEADS, ROWS, ROWS)
                keep = jnp.logical_not(after) if step == 0 else after
                expon = jnp.where(keep, expon, 0.0).reshape(HEADS * ROWS, ROWS)
            mass = mass + (expon[:, :128] + expon[:, 128:])
            mixed = mixed + dot(expon.astype(bf16), v_all[keys, :])
        sums = jnp.sum(mass, axis=-1, keepdims=True)
        mixed = (mixed * (1.0 / sums)).astype(bf16)
        for head in range(HEADS):
            mixed_out = (mixed_mine, mixed_theirs)[head // 2]
            columns = slice((head % 2) * HD, (head % 2 + 1) * HD)
            mixed_out[0, :, columns] = mixed[head * ROWS : (head + 1) * ROWS]
        lse_out[0, 0] = as_row(jnp.log(sums) * LOG2E)

    pl.when(block == 0)(lambda: attend((0,)))
    pl.when(block == 1)(lambda: attend((1, 0)))
    pl.when(block >= 2)(lambda: attend((2, 1, 0)))


def feed_forward_kernel(
    lengths, tok, cot, mixed_mine, mixed_theirs, wide_mine, wide_theirs, deep_mine, deep_theirs,
    gain_ao, gain_fi, gain_fo,
    act_out, gh_out, gm_out, dots_out, fin_out, gres_out, gatt_out,
    inner_mine, inner_theirs, grad_mine, grad_theirs, gains_out, left_s, right_s,
):
    micro, block = pl.program_id(0), pl.program_id(1)
    half_width = wide_mine.shape[1] // 2
    rate, cubic = 0.7978845608028654, 0.044715
    gains = []

    def chain(part):
        here = slice(part * ROWS, (part + 1) * ROWS)
        inputs = tok[0, here].astype(f32)
        place = (block * FFN_ROWS + part * ROWS) + lax.broadcasted_iota(jnp.int32, (ROWS, 1), 0)
        valid = (place < lengths[micro]).astype(f32)
        attended = dot_right(mixed_mine[0, here], deep_mine[:, half_width:]) + dot_right(
            mixed_theirs[0, here], deep_theirs[:, half_width:]
        )
        yield
        hidden = inputs + attended * inverse_rms(attended) * gain_ao[...]
        ffn_in = (hidden * inverse_rms(hidden) * gain_fi[...]).astype(bf16)
        fin_out[0, here] = ffn_in
        result = jnp.zeros(inputs.shape, f32)
        for half in range(2):
            wide = (wide_mine, wide_theirs)[half]
            deep = (deep_mine, deep_theirs)[half]
            inner_out = (inner_mine, inner_theirs)[half]
            for start in range(0, half_width, CHUNK):
                yield
                columns = slice(start, start + CHUNK)
                shifted_columns = slice(half_width + start, half_width + start + CHUNK)
                kept = slice(half * half_width + start, half * half_width + start + CHUNK)
                gate = dot(ffn_in, wide[:, columns])
                up = dot(ffn_in, wide[:, shifted_columns])
                square = gate * gate
                tanh = jnp.tanh(gate * (rate + (rate * cubic) * square))
                side = 0.5 + 0.5 * tanh
                gelu = gate * side
                slope = side + gelu * (1.0 - tanh) * (rate + (3.0 * rate * cubic) * square)
                inner = (gelu * up).astype(bf16)
                inner_out[0, here, columns] = inner
                left_s[here, kept] = (up * slope).astype(bf16)
                right_s[here, kept] = gelu.astype(bf16)
                result = result + dot_right(inner, deep[:, columns])
        yield
        act_out[0, here] = (valid * (hidden + result * inverse_rms(result) * gain_fo[...])).astype(bf16)
        upstream = valid * cot[0, here].astype(f32)
        grad_result, g_fo = norm_back(result, gain_fo[...], upstream)
        grad_result = grad_result.astype(bf16)
        gres_out[0, here] = grad_result
        grad_in = jnp.zeros(inputs.shape, f32)
        for half in range(2):
            wide = (wide_mine, wide_theirs)[half]
            deep = (deep_mine, deep_theirs)[half]
            grad_out = (grad_mine, grad_theirs)[half]
            for start in range(0, half_width, CHUNK):
                yield
                columns = slice(start, start + CHUNK)
                shifted_columns = slice(half_width + start, half_width + start + CHUNK)
                kept = slice(half * half_width + start, half * half_width + start + CHUNK)
                grad_inner = dot(grad_result, deep[:, columns])
                grad_gate = (grad_inner * left_s[here, kept].astype(f32)).astype(bf16)
                grad_up = (grad_inner * right_s[here, kept].astype(f32)).astype(bf16)
                grad_out[0, here, columns] = grad_gate
                grad_out[0, here, shifted_columns] = grad_up
                grad_in = grad_in + dot_right(grad_gate, wide[:, columns])
                grad_in = grad_in + dot_right(grad_up, wide[:, shifted_columns])
        yield
        grad_hidden, g_fi = norm_back(hidden, gain_fi[...], grad_in)
        grad_hidden = upstream + grad_hidden
        gh_out[0, here] = grad_hidden
        grad_att, g_ao = norm_back(attended, gain_ao[...], grad_hidden)
        grad_att = grad_att.astype(bf16)
        gatt_out[0, here] = grad_att
        gains.append((g_ao, g_fi, g_fo))
        yield
        for head in range(HEADS):
            weight, mixed = ((deep_mine, mixed_mine), (deep_theirs, mixed_theirs))[head // 2]
            columns = slice((head % 2) * HD, (head % 2 + 1) * HD)
            out_columns = slice(half_width + columns.start, half_width + columns.stop)
            grad_mixed = dot(grad_att, weight[:, out_columns]).astype(bf16)
            gm_out[0, head, here] = grad_mixed
            product = jnp.sum(grad_mixed.astype(f32) * mixed[0, here, columns].astype(f32), axis=-1, keepdims=True)
            dots_out[0, part, :, head * ROWS : (head + 1) * ROWS] = as_row(product)
        yield

    chains = [chain(part) for part in range(FFN_ROWS // ROWS)]
    next(chains[0])
    for _ in range(5 + 4 * half_width // CHUNK):
        for one in reversed(chains):
            next(one, None)
    for one in chains:
        for _ in one:
            pass

    @pl.when((micro == 0) & (block == 0))
    def _():
        gains_out[...] = jnp.zeros(gains_out.shape, f32)

    for own in gains:
        for row, piece in enumerate(own):
            gains_out[row : row + 1, :] += piece


def attention_backward_kernel(
    qrot, qlin, gm, lse, dots, cos, sin, krot, val, klin, cos_late, sin_late, tok, gh,
    core, mine, theirs, gain_in, gain_q, gain_k,
    input_out, grad_mine, grad_theirs, gains_out, dk, dv, gq_all,
):
    micro, step = pl.program_id(0), pl.program_id(1)

    @pl.when((micro == 0) & (step == 0))
    def _():
        gains_out[...] = jnp.zeros(gains_out.shape, f32)

    def unrotated(grad, cosine, sine):
        return rotate(grad * HD**-0.5, cosine, -sine)

    def attend(backs):
        queries = qrot[0].reshape(HEADS * ROWS, HD)
        grads = gm[0].reshape(HEADS * ROWS, HD)
        after = key_after_query(True)
        after = jnp.concatenate([after] * HEADS, axis=1)
        log_mass, row_dot = lse[0, 0, 0:1], dots[0, 0, 0:1]
        grad_queries = jnp.zeros((HEADS * ROWS, HD), f32)
        for back in backs:
            keys = pl.ds(pl.multiple_of((step - back) * ROWS, ROWS), ROWS)
            key, value = krot[0, keys, :], val[0, keys, :]
            probs = jnp.exp2(dot_right(key, queries) * (LOG2E * HD**-0.5) - log_mass)
            if back != 1:
                probs = jnp.where(jnp.logical_not(after) if back == 0 else after, probs, 0.0)
            grad_probs = dot_right(value, grads)
            grad_scores = (probs * (grad_probs - row_dot)).astype(bf16)
            grad_value = dot(probs.astype(bf16), grads)
            grad_key = dot(grad_scores, queries)
            if back == 0:
                dv[keys, :] = grad_value
                dk[keys, :] = grad_key
            else:
                dv[keys, :] += grad_value
                dk[keys, :] += grad_key
            grad_queries = grad_queries + dot_left(grad_scores, key)
        here = pl.ds(pl.multiple_of(step * ROWS, ROWS), ROWS)
        for head in range(HEADS):
            turned = unrotated(grad_queries[head * ROWS : (head + 1) * ROWS], cos[...], sin[...])
            grad_lin, g_q = norm_back(qlin[0, head], gain_q[...], turned)
            gq_all[here, head * HD : (head + 1) * HD] = grad_lin.astype(bf16)
            gains_out[1:2, :HD] += g_q

    pl.when(step == 0)(lambda: attend((0,)))
    pl.when(step == 1)(lambda: attend((1, 0)))
    pl.when((step == 2) | (step == 3))(lambda: attend((2, 1, 0)))

    @pl.when(step >= 2)
    def _():
        here = pl.ds(pl.multiple_of((step - 2) * ROWS, ROWS), ROWS)
        turned = unrotated(dk[here, :], cos_late[...], sin_late[...])
        grad_key, g_k = norm_back(klin[0], gain_k[...], turned)
        grad_key = grad_key.astype(bf16)
        grad_value = dv[here, :].astype(bf16)
        half = HEADS * HD // 2
        first, second = gq_all[here, :half], gq_all[here, half:]
        grad_mine[0, :, :half] = first
        grad_theirs[0, :, :half] = second
        is_first = jnp.full(grad_key.shape, core[0], jnp.int32) == 0
        grad_mine[0, :, half:] = jnp.where(is_first, grad_key, grad_value)
        grad_theirs[0, :, half:] = jnp.where(is_first, grad_value, grad_key)
        wk, wv = key_and_value(core, mine, theirs)
        grad_in = (
            dot_right(first, mine[:, :half])
            + dot_right(second, theirs[:, :half])
            + dot_right(grad_key, wk)
            + dot_right(grad_value, wv)
        )
        grad_inputs, g_in = norm_back(tok[0].astype(f32), gain_in[...], grad_in)
        input_out[0] = (gh[0] + grad_inputs).astype(bf16)
        gains_out[0:1, :] += g_in
        gains_out[2:3, :HD] += g_k


def whole(array):
    return pl.BlockSpec(array.shape, lambda m, i: (0,) * array.ndim, pipeline_mode=pl.Buffered(1))


def struct(shape, dtype):
    return jax.ShapeDtypeStruct(shape, dtype)


def params(limit):
    return pltpu.CompilerParams(vmem_limit_bytes=limit << 20, dimension_semantics=("arbitrary", "arbitrary"))


def cost(flops, size):
    return pl.CostEstimate(flops=flops, bytes_accessed=size, transcendentals=0)


def rows_spec(width, place=lambda i: i, micro=0):
    return pl.BlockSpec((1, ROWS, width), lambda m, i: (m + micro, place(i), 0))


def heads_spec(place=lambda i: i, micro=0):
    return pl.BlockSpec((1, HEADS, ROWS, HD), lambda m, i: (m + micro, 0, place(i), 0))


def stat_spec(place=lambda i: i, micro=0):
    return pl.BlockSpec((1, 1, 8, HEADS * ROWS), lambda m, i: (m + micro, place(i), 0, 0))


def onward(kernel, inputs, earlier):
    return lambda *refs: kernel(*refs[:inputs], *refs[inputs + earlier :])


def table_spec(place=lambda i: i):
    return pl.BlockSpec((ROWS, HD // 2), lambda m, i: (place(i), 0))


def rope_tables(rows, head_dim):
    half = head_dim // 2
    inverse = 1.0 / rope_base ** (np.arange(half, dtype=np.float32) * np.float32(2.0 / head_dim))
    angle = np.arange(rows, dtype=np.float32)[:, None] * inverse.astype(np.float32)[None, :]
    return jnp.asarray(np.cos(angle), f32), jnp.asarray(np.sin(angle), f32)


def attention_forward(core, tokens, weights, gains, tables, micro, earlier=()):
    micros, rows, width = tokens.shape
    blocks = rows // ROWS
    half = HEADS * HD // 2
    shapes = (
        struct((micros, rows, width), bf16),
        struct((micros, HEADS, rows, HD), f32),
        struct((micros, HEADS, rows, HD), bf16),
        struct((micros, rows, HD), f32),
        struct((micros, rows, HD), bf16),
        struct((micros, rows, HD), bf16),
        struct((micros, rows, half), bf16),
        struct((micros, rows, half), bf16),
        struct((micros, blocks, 8, HEADS * ROWS), f32),
    )
    heads = heads_spec(micro=micro)
    narrow = rows_spec(HD, micro=micro)
    specs = (rows_spec(width, micro=micro), heads, heads, narrow, narrow, narrow) + (
        rows_spec(half, micro=micro),
        rows_spec(half, micro=micro),
        stat_spec(micro=micro),
    )
    operands = (core, tokens, *weights, *gains, *tables)
    return pl.pallas_call(
        onward(attention_forward_kernel, len(operands), len(earlier)),
        grid=(1, blocks),
        in_specs=[pl.BlockSpec(memory_space=pltpu.SMEM), rows_spec(width, micro=micro)] + [whole(w) for w in weights] + [whole(g) for g in gains]
        + [table_spec()] * 2 + [pl.BlockSpec(memory_space=pl.ANY)] * len(earlier),
        out_specs=specs,
        out_shape=shapes,
        scratch_shapes=[pltpu.VMEM((rows, HD), bf16), pltpu.VMEM((rows, HD), bf16)],
        input_output_aliases={len(operands) + i: i for i in range(len(earlier))},
        compiler_params=params(36),
        cost_estimate=cost(5 * 10**9, 20 << 20),
        name="attention_forward",
    )(*operands, *earlier)


def ffn_spec(width):
    return pl.BlockSpec((1, FFN_ROWS, width), lambda m, i: (m, i, 0))


def feed_forward(lengths, tokens, cotangent, mixed, weights, gains):
    micros, rows, width = tokens.shape
    blocks = rows // ROWS
    hidden = weights[0].shape[1] // 2
    shapes = (
        struct((micros, rows, width), bf16),
        struct((micros, rows, width), f32),
        struct((micros, HEADS, rows, HD), bf16),
        struct((micros, blocks, 8, HEADS * ROWS), f32),
        struct((micros, rows, width), bf16),
        struct((micros, rows, width), bf16),
        struct((micros, rows, width), bf16),
    ) + (struct((micros, rows, hidden), bf16),) * 2 + (struct((micros, rows, 2 * hidden), bf16),) * 2 + (
        struct((8, width), f32),
    )
    specs = (
        ffn_spec(width), ffn_spec(width), pl.BlockSpec((1, HEADS, FFN_ROWS, HD), lambda m, i: (m, 0, i, 0)), pl.BlockSpec((1, FFN_ROWS // ROWS, 8, HEADS * ROWS), lambda m, i: (m, i, 0, 0)), ffn_spec(width), ffn_spec(width), ffn_spec(width),
    ) + (ffn_spec(hidden),) * 2 + (ffn_spec(2 * hidden),) * 2 + (
        pl.BlockSpec((8, width), lambda m, i: (0, 0)),
    )
    return pl.pallas_call(
        feed_forward_kernel,
        grid=(micros, rows // FFN_ROWS),
        in_specs=[pl.BlockSpec(memory_space=pltpu.SMEM), ffn_spec(width), ffn_spec(width)]
        + [ffn_spec(HEADS * HD // 2)] * 2
        + [whole(w) for w in weights]
        + [whole(g) for g in gains],
        out_specs=specs,
        out_shape=shapes,
        scratch_shapes=[pltpu.VMEM((FFN_ROWS, 2 * hidden), bf16), pltpu.VMEM((FFN_ROWS, 2 * hidden), bf16)],
        compiler_params=params(56),
        cost_estimate=cost(38 * 10**9, 80 << 20),
        name="feed_forward",
    )(lengths, tokens, cotangent, *mixed, *weights, *gains)


def attention_backward(core, saved, grads, tokens, weights, gains, tables, micro, earlier=()):
    _, qlin, qrot, klin, krot, value, _, _, lse = saved
    grad_hidden, grad_mixed, dots = grads
    micros, rows, width = tokens.shape
    blocks = rows // ROWS
    half = HEADS * HD // 2

    def early(i):
        return jnp.minimum(i, blocks - 1)

    def late(i):
        return jnp.maximum(i - 2, 0)

    keys = pl.BlockSpec((1, rows, HD), lambda m, i: (m + micro, 0, 0))
    shapes = (
        struct((micros, rows, width), bf16),
        struct((micros, rows, half + HD), bf16),
        struct((micros, rows, half + HD), bf16),
        struct((8, width), f32),
    )
    specs = tuple(rows_spec(size, late, micro) for size in (width, half + HD, half + HD)) + (
        pl.BlockSpec((8, width), lambda m, i: (0, 0)),
    )
    operands = (
        qrot, qlin, grad_mixed, lse, dots, *tables, krot, value, klin, *tables, tokens, grad_hidden, core, *weights, *gains,
    )
    return pl.pallas_call(
        onward(attention_backward_kernel, len(operands), len(earlier)),
        grid=(1, blocks + 2),
        in_specs=[heads_spec(early, micro)] * 3 + [stat_spec(early, micro)] * 2 + [table_spec(early)] * 2 + [keys] * 2
        + [rows_spec(HD, late, micro)] + [table_spec(late)] * 2 + [rows_spec(width, late, micro)] * 2
        + [pl.BlockSpec(memory_space=pltpu.SMEM)] + [whole(w) for w in weights] + [whole(g) for g in gains]
        + [pl.BlockSpec(memory_space=pl.ANY)] * len(earlier),
        out_specs=specs,
        out_shape=shapes,
        scratch_shapes=[pltpu.VMEM((rows, HD), f32), pltpu.VMEM((rows, HD), f32), pltpu.VMEM((rows, HEADS * HD), bf16)],
        input_output_aliases={len(operands) + i: i for i in range(len(earlier))},
        compiler_params=params(36),
        cost_estimate=cost(9 * 10**9, 20 << 20),
        name="attention_backward",
    )(*operands, *earlier)


def weight_grad(left, right):
    return dot_left(left.reshape(-1, left.shape[-1]), right.reshape(-1, right.shape[-1])).astype(bf16)


def fold(operands, groups, scalars, grid, outs):
    flat_terms = [term for group in groups for columns in group for term in columns]

    def kernel(_, *refs):
        sources, targets = refs[: len(flat_terms)], refs[len(flat_terms) :]
        at = 0
        for group, target in zip(groups, targets):
            start = 0
            for columns in group:
                value = sources[at][...].astype(f32)
                for more in range(1, len(columns)):
                    value = value + sources[at + more][...].astype(f32)
                width = value.shape[-1]
                target[..., start : start + width] = value.reshape(target.shape[:-1] + (width,)).astype(target.dtype)
                start += width
                at += len(columns)

    return pl.pallas_call(
        kernel,
        grid_spec=pltpu.PrefetchScalarGridSpec(
            num_scalar_prefetch=1,
            grid=grid,
            in_specs=[pl.BlockSpec(block, index) for _, block, index in flat_terms],
            out_specs=tuple(pl.BlockSpec(block, index) for _, block, index, _ in outs),
        ),
        out_shape=tuple(struct(shape, kind) for shape, _, _, kind in outs),
        compiler_params=pltpu.CompilerParams(vmem_limit_bytes=24 << 20, dimension_semantics=("arbitrary",)),
        cost_estimate=cost(10**6, 8 << 20),
        name="fold",
    )(scalars, *[operands[i] for i, _, _ in flat_terms])


def factors(count):
    side = 1
    while 2 * side**3 < count:
        side += 1
    return (2 * side, side, side) if 2 * side**3 == count else (count, 1, 1)


def place(sizes, axis):
    index = lax.axis_index("fsdp")
    for size in sizes[axis + 1 :]:
        index = index // size
    return index % sizes[axis]


def shifted(sizes, axis, step):
    stride = 1
    for size in sizes[axis + 1 :]:
        stride *= size
    pairs = []
    for index in range(sizes[0] * sizes[1] * sizes[2]):
        at = (index // stride) % sizes[axis]
        pairs.append((index, index + ((at + step) % sizes[axis] - at) * stride))
    return pairs


def tie(*trees):
    return lax.optimization_barrier(trees)


def ring_pairs(sizes, turn, step):
    pairs = []
    for core in range(2):
        axis = 1 if (core == 0) == (turn == 0) else 2
        pairs += [(2 * source + core, 2 * target + core) for source, target in shifted(sizes, axis, step)]
    return pairs


def place_at(sizes, turn, core):
    first, second = place(sizes, 1), place(sizes, 2)
    return jnp.where(core == 0, first, second) if turn == 0 else jnp.where(core == 0, second, first)


def sent_turn(block, sizes, turn):
    return [block] + [
        lax.ppermute(block, ("fsdp", "dp"), ring_pairs(sizes, turn, step)) for step in range(1, sizes[1])
    ]


def sent_z(block, sizes):
    return [block] + [lax.ppermute(block, "fsdp", shifted(sizes, 0, step)) for step in range(1, sizes[0])]


def joined_z(pieces, sizes):
    here, size = place(sizes, 0), sizes[0]
    rows = []
    for at in range(size):
        row = pieces[-1]
        for step in range(size - 1):
            row = jnp.where((here - at) % size == step, pieces[step], row)
        rows.append(row)
    return jnp.stack(rows)


def sent_middle(block, sizes, core):
    return sent_turn(block, sizes, 0)


def joined_middle(pieces, sizes, core):
    here, side = place_at(sizes, 0, core), sizes[1]
    if side == 1:
        return pieces[0][:, None]
    if side == 2:
        own, other = pieces
        return jnp.stack([jnp.where(here == 0, own, other), jnp.where(here == 0, other, own)], axis=1)
    out = jnp.zeros(pieces[0].shape[:1] + (side,) + pieces[0].shape[1:], pieces[0].dtype)
    for step, piece in enumerate(pieces):
        out = lax.dynamic_update_slice_in_dim(out, piece[:, None], (here - step) % side, 1)
    return out


def sent_last(block, sizes, core):
    return sent_turn(block, sizes, 1)


def joined_last(pieces, sizes, core):
    here, side = place_at(sizes, 1, core), sizes[1]
    if side == 2:
        own, other = pieces
        low = jnp.where(here == 0, own, other)
        high = jnp.where(here == 0, other, own)
        cross = [jnp.where(core == 0, high[:, 0], low[:, 1]), jnp.where(core == 0, low[:, 1], high[:, 0])]
        return jnp.stack([low[:, 0], cross[0], cross[1], high[:, 1]], axis=1)
    out = jnp.zeros(pieces[0].shape[:1] + (side * side,) + pieces[0].shape[2:], pieces[0].dtype)
    for step, piece in enumerate(pieces):
        there = (here - step) % side
        for k in range(side):
            at = jnp.where(core == 0, side * k + there, side * there + k)
            out = lax.dynamic_update_slice_in_dim(out, piece[:, k : k + 1], at, 1)
    return out


def gather_middle(block, sizes, core):
    return joined_middle(sent_middle(block, sizes, core), sizes, core)


def gather_last(block, sizes, core):
    return joined_last(sent_last(block, sizes, core), sizes, core)


def flat(block):
    return block.reshape(-1, block.shape[-1])


def swap(block):
    return lax.ppermute(block, "dp", [(0, 1), (1, 0)])


def total(parts):
    out = parts[0].astype(jnp.float32)
    for part in parts[1:]:
        out = out + part.astype(jnp.float32)
    return out


def boxed(mine, arrived, sizes):
    box = (sizes[0], sizes[1] * sizes[2], mine.shape[0] // (sizes[0] * sizes[1] * sizes[2]), mine.shape[1])
    return [mine.reshape(box)] + ([] if arrived is None else [arrived.reshape(box)])


def moved(sent, sizes, turn):
    return [
        lax.ppermute(piece, ("fsdp", "dp"), ring_pairs(sizes, turn, step)) for step, piece in enumerate(sent, 1)
    ]


def moved_z(sent, sizes):
    return [lax.ppermute(piece, "fsdp", shifted(sizes, 0, step)) for step, piece in enumerate(sent, 1)]


def fold_first(bundle, sizes, core):
    here, side = place_at(sizes, 1, core), sizes[1]
    places = []
    for step in range(side):
        there = (here + step) % side
        places += [jnp.where(core == 0, side * k + there, side * there + k) for k in range(side)]
    box = bundle[0][0].shape
    width = sum(parts[0].shape[-1] for parts in bundle)
    operands, groups, outs = [], [], []
    for step in range(side):
        group = []
        for parts in bundle:
            block = (box[0], 1, box[2], parts[0].shape[-1])
            columns = []
            for part in parts:
                operands.append(part)
                columns.append((len(operands) - 1, block, lambda k, at, step=step: (0, at[step * side + k], 0, 0)))
            group.append(columns)
        groups.append(group)
        outs.append(
            (
                (box[0], side, box[2], width),
                (box[0], 1, box[2], width),
                lambda k, at: (0, k, 0, 0),
                bf16 if step else f32,
            )
        )
    keep, *sent = fold(operands, groups, jnp.stack(places).astype(jnp.int32), (side,), outs)
    return keep, sent


def fold_middle(bundle, sizes, core):
    here, side = place_at(sizes, 0, core), sizes[1]
    box = bundle[0][0].shape
    width = sum(parts[0].shape[-1] for parts in bundle)
    operands, groups, outs = [], [], []
    for step in range(side):
        group = []
        for parts in bundle:
            block = (1, 1, box[2], parts[0].shape[-1])
            columns = []
            for part in parts:
                operands.append(part)
                columns.append((len(operands) - 1, block, lambda z, at, step=step: (z, at[step], 0, 0)))
            group.append(columns)
        groups.append(group)
        outs.append(
            ((box[0], box[2], width), (1, box[2], width), lambda z, at: (z, 0, 0), bf16 if step else f32)
        )
    places = jnp.stack([(here + step) % side for step in range(side)]).astype(jnp.int32)
    keep, *sent = fold(operands, groups, places, (box[0],), outs)
    return keep, sent


def fold_z(parts, sizes):
    here, size = place(sizes, 0), sizes[0]
    _, rows, width = parts[0].shape
    groups, outs = [], []
    for step in range(size):
        groups.append(
            [[(i, (1, rows, width), lambda z, at, step=step: (at[step], 0, 0)) for i in range(len(parts))]]
        )
        outs.append(((rows, width), (rows, width), lambda z, at: (0, 0), bf16 if step else f32))
    places = jnp.stack([(here + step) % size for step in range(size)]).astype(jnp.int32)
    keep, *sent = fold(parts, groups, places, (1,), outs)
    return keep, sent


def half_of(array, core, axis):
    size = array.shape[axis] // 2
    return lax.dynamic_slice_in_dim(array, core * size, size, axis)


def in_order(core, mine, theirs):
    return jnp.concatenate([jnp.where(core == 0, mine, theirs), jnp.where(core == 0, theirs, mine)], axis=1)


def pack_gains(pieces, rows):
    columns = [jnp.pad(piece, (0, rows - piece.shape[0])) for piece in pieces]
    return jnp.pad(jnp.stack(columns, axis=1), ((0, 0), (0, 128 - len(columns))))


def pack_gain_grads(pieces, count, rows):
    columns = [
        jnp.pad(piece.reshape(count, -1), ((0, 0), (0, rows - piece.shape[0] // count))).reshape(-1)
        for piece in pieces
    ]
    return jnp.pad(jnp.stack(columns, axis=1), ((0, 0), (0, 128 - len(columns))))


def local(
    sizes,
    tokens,
    cotangent,
    seq_lengths,
    slot_of,
    w_query,
    w_key,
    w_value,
    w_out,
    w_gate,
    w_up,
    w_down,
    gain_attn_in,
    gain_query,
    gain_key,
    gain_attn_out,
    gain_ffn_in,
    gain_ffn_out,
):
    micro_count = tokens.shape[0]
    count = lax.axis_size("fsdp")
    devices = count * lax.axis_size("dp")
    core = lax.axis_index("dp")
    device = lax.axis_index("fsdp") * lax.axis_size("dp") + core
    slots = jnp.arange(micro_count, dtype=jnp.int32) * devices + device
    lengths = jnp.sum(
        jnp.where(slot_of[None, :] == slots[:, None], seq_lengths[None, :], 0), axis=1
    )
    rows = w_query.shape[0]
    gains = (gain_attn_in, gain_query, gain_key, gain_attn_out, gain_ffn_in, gain_ffn_out)
    gain_rows = tuple(piece.shape[0] for piece in gains)

    half, hidden = HEADS * HD // 2, w_gate.shape[1] // 2
    first = jnp.concatenate(
        [half_of(w_query, core, 1), jnp.where(core == 0, w_key, w_value), pack_gains(gains, rows)], axis=1
    )
    wide = jnp.concatenate([half_of(w_gate, core, 1), half_of(w_up, core, 1)], axis=1)
    deep = jnp.concatenate([half_of(w_down, core, 0).T, half_of(w_out, core, 0).T], axis=1)
    first = sent_z(first, sizes)
    first, wide = tie(first, wide)
    wide = sent_z(wide, sizes)
    first = flat(gather_last(gather_middle(joined_z(first, sizes), sizes, core), sizes, core))
    first, wide = tie(first, wide)
    wide, deep = tie(wide, deep)
    deep = sent_z(deep, sizes)
    attn_weights = (first, swap(first))
    full_gains = [
        first[:, half + HD + i].reshape(count, rows)[:, :size].reshape(1, -1).astype(f32)
        for i, size in enumerate(gain_rows)
    ]
    tables = rope_tables(tokens.shape[1], HD)
    which = jnp.reshape(core, (1,)).astype(jnp.int32)
    wide = joined_z(wide, sizes)
    wide, attn_weights = tie(wide, attn_weights)
    wide = sent_middle(wide, sizes, core)
    saved = attention_forward(which, tokens, attn_weights, full_gains[:3], tables, 0)
    wide, deep, saved = tie(wide, deep, saved)
    wide, deep = joined_middle(wide, sizes, core), joined_z(deep, sizes)
    wide, deep, saved = tie(wide, deep, saved)
    deep, wide = sent_middle(deep, sizes, core), sent_last(wide, sizes, core)
    for micro in range(1, micro_count):
        saved = attention_forward(which, tokens, attn_weights, full_gains[:3], tables, micro, saved)
    deep, saved = tie(deep, saved)
    deep = joined_middle(deep, sizes, core)
    wide, deep = tie(wide, deep)
    deep = sent_last(deep, sizes, core)
    wide = flat(joined_last(wide, sizes, core))
    wide_swapped = swap(wide)
    deep = flat(joined_last(deep, sizes, core))
    ffn_weights = (wide, wide_swapped, deep, swap(deep))

    mixed = saved[6:8]
    (
        outputs, grad_hidden, grad_mixed, dots, ffn_in, grad_result, grad_att,
        inner_mine, inner_theirs, grad_mine, grad_theirs, gains_ffn,
    ) = feed_forward(lengths, tokens, cotangent, mixed, ffn_weights, full_gains[3:])
    wide = weight_grad(ffn_in, grad_theirs)
    wide, grad_mine = tie(wide, grad_mine)
    wide_arrived = swap(wide)
    wide = weight_grad(ffn_in, grad_mine)
    wide_keep, wide_sent = fold_first([boxed(wide, wide_arrived, sizes)], sizes, core)
    wide_sent, grad_mixed = tie(wide_sent, grad_mixed)
    wide_arrived = moved(wide_sent, sizes, 1)
    for micro in range(micro_count):
        *back, gains_own = attention_backward(
            which, saved, (grad_hidden, grad_mixed, dots), tokens, attn_weights, full_gains[:3], tables,
            micro, back if micro else (),
        )
        gains_attn = gains_attn + gains_own if micro else gains_own
        if micro == 0:
            wide_arrived, back, inner_theirs, grad_att = tie(wide_arrived, back, inner_theirs, grad_att)
            wide_keep, wide_sent = fold_middle([[wide_keep, *wide_arrived]], sizes, core)
            wide_sent, back, inner_theirs, grad_att = tie(wide_sent, back, inner_theirs, grad_att)
            wide_arrived = moved(wide_sent, sizes, 0)
            deep = [weight_grad(grad_result, inner_theirs), weight_grad(grad_att, mixed[1])]
            deep, inner_mine, grad_att = tie(deep, inner_mine, grad_att)
            deep_arrived = [swap(piece) for piece in deep]
            deep = [weight_grad(grad_result, inner_mine), weight_grad(grad_att, mixed[0])]
            deep = [boxed(own, piece, sizes) for own, piece in zip(deep, deep_arrived)]
            deep_keep, deep_sent = fold_first(deep, sizes, core)
            wide_arrived, deep_sent, back = tie(wide_arrived, deep_sent, back)
            wide_keep, wide_sent = fold_z([wide_keep, *wide_arrived], sizes)
            wide_sent, deep_sent, back = tie(wide_sent, deep_sent, back)
            deep_arrived, wide_arrived = moved(deep_sent, sizes, 1), moved_z(wide_sent, sizes)
    wide_arrived, deep_arrived, back = tie(wide_arrived, deep_arrived, back)
    deep_keep, deep_sent = fold_middle([[deep_keep, *deep_arrived]], sizes, core)
    deep_sent, back = tie(deep_sent, back)
    deep_arrived = moved(deep_sent, sizes, 0)
    input_grad, grad_mine, grad_theirs = back
    gain_grads = (
        gains_attn[0], gains_attn[1, :HD], gains_attn[2, :HD], gains_ffn[0], gains_ffn[1], gains_ffn[2],
    )
    gain_block = pack_gain_grads(gain_grads, count, rows).astype(bf16)
    normed = saved[0]
    d_theirs = weight_grad(normed, grad_theirs)
    d_theirs, grad_mine = tie(d_theirs, grad_mine)
    d_mine = weight_grad(normed, grad_mine)
    narrow = [boxed(d_mine, swap(d_theirs), sizes), boxed(gain_block, None, sizes)]
    narrow_keep, narrow_sent = fold_first(narrow, sizes, core)
    deep_arrived, narrow_sent = tie(deep_arrived, narrow_sent)
    deep_keep, deep_sent = fold_z([deep_keep, *deep_arrived], sizes)
    deep_sent, narrow_sent = tie(deep_sent, narrow_sent)
    narrow_arrived, deep_arrived = moved(narrow_sent, sizes, 1), moved_z(deep_sent, sizes)
    narrow_keep, narrow_sent = fold_middle([[narrow_keep, *narrow_arrived]], sizes, core)
    narrow_arrived = moved(narrow_sent, sizes, 0)
    deep_arrived, narrow_arrived = tie(deep_arrived, narrow_arrived)
    narrow_keep, narrow_sent = fold_z([narrow_keep, *narrow_arrived], sizes)
    narrow_arrived = moved_z(narrow_sent, sizes)
    early = jnp.concatenate([total([wide_keep, *wide_arrived]), total([deep_keep, *deep_arrived])], axis=1)
    early_theirs = swap(early)

    def shard(mine, theirs, start, width):
        return in_order(core, mine[:, start : start + width], theirs[:, start : start + width])

    starts = ((0, hidden), (hidden, hidden), (2 * hidden, hidden), (3 * hidden, half))
    shards = [shard(early, early_theirs, *place) for place in starts]
    shards, narrow_arrived = tie(shards, narrow_arrived)
    narrow = total([narrow_keep, *narrow_arrived])
    narrow_theirs = swap(narrow)
    keyval = shard(narrow, narrow_theirs, half, HD)
    gain_sums = narrow[:, half + HD :] + narrow_theirs[:, half + HD :]
    return (
        outputs,
        input_grad,
        shard(narrow, narrow_theirs, 0, half),
        keyval[:, :HD],
        keyval[:, HD:],
        shards[3].T,
        shards[0],
        shards[1],
        shards[2].T,
    ) + tuple(gain_sums[:size, i] for i, size in enumerate(gain_rows))


def solution(mesh):
    sizes = factors(mesh.shape["fsdp"])
    in_specs = (
        P(None, ("fsdp", "dp"), None),
        P(None, ("fsdp", "dp"), None),
        P(),
        P(),
        P("fsdp", None),
        P("fsdp", None),
        P("fsdp", None),
        P(None, "fsdp"),
        P("fsdp", None),
        P("fsdp", None),
        P(None, "fsdp"),
        P("fsdp"),
        P("fsdp"),
        P("fsdp"),
        P("fsdp"),
        P("fsdp"),
        P("fsdp"),
    )
    out_specs = (
        P(None, ("fsdp", "dp"), None),
        P(None, ("fsdp", "dp"), None),
        P("fsdp", None),
        P("fsdp", None),
        P("fsdp", None),
        P(None, "fsdp"),
        P("fsdp", None),
        P("fsdp", None),
        P(None, "fsdp"),
        P("fsdp"),
        P("fsdp"),
        P("fsdp"),
        P("fsdp"),
        P("fsdp"),
        P("fsdp"),
    )
    return jax.shard_map(functools.partial(local, sizes), mesh=mesh, in_specs=in_specs, out_specs=out_specs, check_vma=False)
```

```python
import functools

import jax
import jax.numpy as jnp
import numpy as np
from jax import lax
from jax.experimental import pallas as pl
from jax.experimental.pallas import tpu as pltpu
from jax.sharding import PartitionSpec as P

HEADS = 4
HD = 256
norm_eps = 1e-06
rope_base = 10000.0
ROWS = 256
FFN_ROWS = 512
CHUNK = 1024
LOG2E = 1.4426950408889634
f32 = jnp.float32
bf16 = jnp.bfloat16


def dot(left, right):
    return jnp.dot(left, right, preferred_element_type=f32)


def dot_right(left, right):
    return lax.dot_general(left, right, (((1,), (1,)), ((), ())), preferred_element_type=f32)


def dot_left(left, right):
    return lax.dot_general(left, right, (((0,), (0,)), ((), ())), preferred_element_type=f32)


def inverse_rms(value):
    return lax.rsqrt(jnp.mean(value * value, axis=-1, keepdims=True) + norm_eps)


def norm_back(value, gain, grad):
    scale = inverse_rms(value)
    unit = value * scale
    weighted = gain * grad
    inner = jnp.mean(unit * weighted, axis=-1, keepdims=True)
    return scale * (weighted - unit * inner), jnp.sum(unit * grad, axis=0, keepdims=True)


def rotate(value, cosine, sine):
    half = value.shape[-1] // 2
    first = value[:, :half]
    second = value[:, half:]
    return jnp.concatenate([first * cosine - second * sine, second * cosine + first * sine], axis=1)


def as_row(column):
    return jnp.transpose(jnp.broadcast_to(column, (column.shape[0], 128)))[:8]


def key_after_query(transposed):
    shape = (ROWS, ROWS)
    query = lax.broadcasted_iota(jnp.int32, shape, 1 if transposed else 0)
    key = lax.broadcasted_iota(jnp.int32, shape, 0 if transposed else 1)
    return key > query


def key_and_value(core, mine, theirs):
    half = HEADS * HD // 2
    left, right = mine[:, half : half + HD], theirs[:, half : half + HD]
    first = jnp.full(left.shape, core[0], jnp.int32) == 0
    return jnp.where(first, left, right), jnp.where(first, right, left)


def attention_forward_kernel(
    core, tok, mine, theirs, gain_in, gain_q, gain_k, cos, sin,
    a_out, qlin_out, qrot_out, klin_out, krot_out, v_out, mixed_mine, mixed_theirs, lse_out, k_all, v_all,
):
    block = pl.program_id(1)
    inputs = tok[0].astype(f32)
    normed = (inputs * inverse_rms(inputs) * gain_in[...]).astype(bf16)
    a_out[0] = normed
    cosine, sine = cos[...], sin[...]

    def prepared(linear, gain):
        return rotate(linear * inverse_rms(linear) * gain, cosine, sine).astype(bf16)

    here = pl.ds(pl.multiple_of(block * ROWS, ROWS), ROWS)
    wk, wv = key_and_value(core, mine, theirs)
    key_lin = dot(normed, wk)
    klin_out[0] = key_lin
    key_rot = prepared(key_lin, gain_k[...])
    krot_out[0] = key_rot
    k_all[here, :] = key_rot
    value = dot(normed, wv).astype(bf16)
    v_out[0] = value
    v_all[here, :] = value
    for half, weight in enumerate((mine, theirs)):
        linear = dot(normed, weight[:, : HEADS * HD // 2])
        for head in range(2):
            part = linear[:, head * HD : (head + 1) * HD]
            qlin_out[0, 2 * half + head] = part
            qrot_out[0, 2 * half + head] = prepared(part, gain_q[...])

    def attend(steps):
        queries = qrot_out[0].reshape(HEADS * ROWS, HD)
        after = key_after_query(False)[None]
        mass = jnp.zeros((HEADS * ROWS, 128), f32)
        mixed = jnp.zeros((HEADS * ROWS, HD), f32)
        for step in steps:
            keys = pl.ds(pl.multiple_of((block - step) * ROWS, ROWS), ROWS)
            expon = jnp.exp2(dot_right(queries, k_all[keys, :]) * (LOG2E * HD**-0.5))
            if step != 1:
                expon = expon.reshape(HEADS, ROWS, ROWS)
                keep = jnp.logical_not(after) if step == 0 else after
                expon = jnp.where(keep, expon, 0.0).reshape(HEADS * ROWS, ROWS)
            mass = mass + (expon[:, :128] + expon[:, 128:])
            mixed = mixed + dot(expon.astype(bf16), v_all[keys, :])
        sums = jnp.sum(mass, axis=-1, keepdims=True)
        mixed = (mixed * (1.0 / sums)).astype(bf16)
        for head in range(HEADS):
            mixed_out = (mixed_mine, mixed_theirs)[head // 2]
            columns = slice((head % 2) * HD, (head % 2 + 1) * HD)
            mixed_out[0, :, columns] = mixed[head * ROWS : (head + 1) * ROWS]
        lse_out[0, 0] = as_row(jnp.log(sums) * LOG2E)

    pl.when(block == 0)(lambda: attend((0,)))
    pl.when(block == 1)(lambda: attend((1, 0)))
    pl.when(block >= 2)(lambda: attend((2, 1, 0)))


def feed_forward_kernel(
    lengths, tok, cot, mixed_mine, mixed_theirs, wide_mine, wide_theirs, deep_mine, deep_theirs,
    gain_ao, gain_fi, gain_fo,
    act_out, gh_out, gm_out, dots_out, fin_out, gres_out, gatt_out,
    inner_mine, inner_theirs, grad_mine, grad_theirs, gains_out, left_s, right_s,
):
    micro, block = pl.program_id(0), pl.program_id(1)
    half_width = wide_mine.shape[1] // 2
    rate, cubic = 0.7978845608028654, 0.044715
    gains = []

    def chain(part):
        here = slice(part * ROWS, (part + 1) * ROWS)
        inputs = tok[0, here].astype(f32)
        place = (block * FFN_ROWS + part * ROWS) + lax.broadcasted_iota(jnp.int32, (ROWS, 1), 0)
        valid = (place < lengths[micro]).astype(f32)
        attended = dot_right(mixed_mine[0, here], deep_mine[:, half_width:]) + dot_right(
            mixed_theirs[0, here], deep_theirs[:, half_width:]
        )
        yield
        hidden = inputs + attended * inverse_rms(attended) * gain_ao[...]
        ffn_in = (hidden * inverse_rms(hidden) * gain_fi[...]).astype(bf16)
        fin_out[0, here] = ffn_in
        result = jnp.zeros(inputs.shape, f32)
        for half in range(2):
            wide = (wide_mine, wide_theirs)[half]
            deep = (deep_mine, deep_theirs)[half]
            inner_out = (inner_mine, inner_theirs)[half]
            for start in range(0, half_width, CHUNK):
                yield
                columns = slice(start, start + CHUNK)
                shifted_columns = slice(half_width + start, half_width + start + CHUNK)
                kept = slice(half * half_width + start, half * half_width + start + CHUNK)
                gate = dot(ffn_in, wide[:, columns])
                up = dot(ffn_in, wide[:, shifted_columns])
                square = gate * gate
                tanh = jnp.tanh(gate * (rate + (rate * cubic) * square))
                side = 0.5 + 0.5 * tanh
                gelu = gate * side
                slope = side + gelu * (1.0 - tanh) * (rate + (3.0 * rate * cubic) * square)
                inner = (gelu * up).astype(bf16)
                inner_out[0, here, columns] = inner
                left_s[here, kept] = (up * slope).astype(bf16)
                right_s[here, kept] = gelu.astype(bf16)
                result = result + dot_right(inner, deep[:, columns])
        yield
        act_out[0, here] = (valid * (hidden + result * inverse_rms(result) * gain_fo[...])).astype(bf16)
        upstream = valid * cot[0, here].astype(f32)
        grad_result, g_fo = norm_back(result, gain_fo[...], upstream)
        grad_result = grad_result.astype(bf16)
        gres_out[0, here] = grad_result
        grad_in = jnp.zeros(inputs.shape, f32)
        for half in range(2):
            wide = (wide_mine, wide_theirs)[half]
            deep = (deep_mine, deep_theirs)[half]
            grad_out = (grad_mine, grad_theirs)[half]
            for start in range(0, half_width, CHUNK):
                yield
                columns = slice(start, start + CHUNK)
                shifted_columns = slice(half_width + start, half_width + start + CHUNK)
                kept = slice(half * half_width + start, half * half_width + start + CHUNK)
                grad_inner = dot(grad_result, deep[:, columns])
                grad_gate = (grad_inner * left_s[here, kept].astype(f32)).astype(bf16)
                grad_up = (grad_inner * right_s[here, kept].astype(f32)).astype(bf16)
                grad_out[0, here, columns] = grad_gate
                grad_out[0, here, shifted_columns] = grad_up
                grad_in = grad_in + dot_right(grad_gate, wide[:, columns])
                grad_in = grad_in + dot_right(grad_up, wide[:, shifted_columns])
        yield
        grad_hidden, g_fi = norm_back(hidden, gain_fi[...], grad_in)
        grad_hidden = upstream + grad_hidden
        gh_out[0, here] = grad_hidden
        grad_att, g_ao = norm_back(attended, gain_ao[...], grad_hidden)
        grad_att = grad_att.astype(bf16)
        gatt_out[0, here] = grad_att
        gains.append((g_ao, g_fi, g_fo))
        yield
        for head in range(HEADS):
            weight, mixed = ((deep_mine, mixed_mine), (deep_theirs, mixed_theirs))[head // 2]
            columns = slice((head % 2) * HD, (head % 2 + 1) * HD)
            out_columns = slice(half_width + columns.start, half_width + columns.stop)
            grad_mixed = dot(grad_att, weight[:, out_columns]).astype(bf16)
            gm_out[0, head, here] = grad_mixed
            product = jnp.sum(grad_mixed.astype(f32) * mixed[0, here, columns].astype(f32), axis=-1, keepdims=True)
            dots_out[0, part, :, head * ROWS : (head + 1) * ROWS] = as_row(product)
        yield

    chains = [chain(part) for part in range(FFN_ROWS // ROWS)]
    next(chains[0])
    for _ in range(5 + 4 * half_width // CHUNK):
        for one in reversed(chains):
            next(one, None)
    for one in chains:
        for _ in one:
            pass

    @pl.when((micro == 0) & (block == 0))
    def _():
        gains_out[...] = jnp.zeros(gains_out.shape, f32)

    for own in gains:
        for row, piece in enumerate(own):
            gains_out[row : row + 1, :] += piece


def attention_backward_kernel(
    qrot, qlin, gm, lse, dots, cos, sin, krot, val, klin, cos_late, sin_late, tok, gh,
    core, mine, theirs, gain_in, gain_q, gain_k,
    input_out, grad_mine, grad_theirs, gains_out, dk, dv, gq_all,
):
    micro, step = pl.program_id(0), pl.program_id(1)

    @pl.when((micro == 0) & (step == 0))
    def _():
        gains_out[...] = jnp.zeros(gains_out.shape, f32)

    def unrotated(grad, cosine, sine):
        return rotate(grad * HD**-0.5, cosine, -sine)

    def attend(backs):
        queries = qrot[0].reshape(HEADS * ROWS, HD)
        grads = gm[0].reshape(HEADS * ROWS, HD)
        after = key_after_query(True)
        after = jnp.concatenate([after] * HEADS, axis=1)
        log_mass, row_dot = lse[0, 0, 0:1], dots[0, 0, 0:1]
        grad_queries = jnp.zeros((HEADS * ROWS, HD), f32)
        for back in backs:
            keys = pl.ds(pl.multiple_of((step - back) * ROWS, ROWS), ROWS)
            key, value = krot[0, keys, :], val[0, keys, :]
            probs = jnp.exp2(dot_right(key, queries) * (LOG2E * HD**-0.5) - log_mass)
            if back != 1:
                probs = jnp.where(jnp.logical_not(after) if back == 0 else after, probs, 0.0)
            grad_probs = dot_right(value, grads)
            grad_scores = (probs * (grad_probs - row_dot)).astype(bf16)
            grad_value = dot(probs.astype(bf16), grads)
            grad_key = dot(grad_scores, queries)
            if back == 0:
                dv[keys, :] = grad_value
                dk[keys, :] = grad_key
            else:
                dv[keys, :] += grad_value
                dk[keys, :] += grad_key
            grad_queries = grad_queries + dot_left(grad_scores, key)
        here = pl.ds(pl.multiple_of(step * ROWS, ROWS), ROWS)
        for head in range(HEADS):
            turned = unrotated(grad_queries[head * ROWS : (head + 1) * ROWS], cos[...], sin[...])
            grad_lin, g_q = norm_back(qlin[0, head], gain_q[...], turned)
            gq_all[here, head * HD : (head + 1) * HD] = grad_lin.astype(bf16)
            gains_out[1:2, :HD] += g_q

    pl.when(step == 0)(lambda: attend((0,)))
    pl.when(step == 1)(lambda: attend((1, 0)))
    pl.when((step == 2) | (step == 3))(lambda: attend((2, 1, 0)))

    @pl.when(step >= 2)
    def _():
        here = pl.ds(pl.multiple_of((step - 2) * ROWS, ROWS), ROWS)
        turned = unrotated(dk[here, :], cos_late[...], sin_late[...])
        grad_key, g_k = norm_back(klin[0], gain_k[...], turned)
        grad_key = grad_key.astype(bf16)
        grad_value = dv[here, :].astype(bf16)
        half = HEADS * HD // 2
        first, second = gq_all[here, :half], gq_all[here, half:]
        grad_mine[0, :, :half] = first
        grad_theirs[0, :, :half] = second
        is_first = jnp.full(grad_key.shape, core[0], jnp.int32) == 0
        grad_mine[0, :, half:] = jnp.where(is_first, grad_key, grad_value)
        grad_theirs[0, :, half:] = jnp.where(is_first, grad_value, grad_key)
        wk, wv = key_and_value(core, mine, theirs)
        grad_in = (
            dot_right(first, mine[:, :half])
            + dot_right(second, theirs[:, :half])
            + dot_right(grad_key, wk)
            + dot_right(grad_value, wv)
        )
        grad_inputs, g_in = norm_back(tok[0].astype(f32), gain_in[...], grad_in)
        input_out[0] = (gh[0] + grad_inputs).astype(bf16)
        gains_out[0:1, :] += g_in
        gains_out[2:3, :HD] += g_k


def whole(array):
    return pl.BlockSpec(array.shape, lambda m, i: (0,) * array.ndim, pipeline_mode=pl.Buffered(1))


def struct(shape, dtype):
    return jax.ShapeDtypeStruct(shape, dtype)


def params(limit):
    return pltpu.CompilerParams(vmem_limit_bytes=limit << 20, dimension_semantics=("arbitrary", "arbitrary"))


def cost(flops, size):
    return pl.CostEstimate(flops=flops, bytes_accessed=size, transcendentals=0)


def rows_spec(width, place=lambda i: i, micro=0):
    return pl.BlockSpec((1, ROWS, width), lambda m, i: (m + micro, place(i), 0))


def heads_spec(place=lambda i: i, micro=0):
    return pl.BlockSpec((1, HEADS, ROWS, HD), lambda m, i: (m + micro, 0, place(i), 0))


def stat_spec(place=lambda i: i, micro=0):
    return pl.BlockSpec((1, 1, 8, HEADS * ROWS), lambda m, i: (m + micro, place(i), 0, 0))


def onward(kernel, inputs, earlier):
    return lambda *refs: kernel(*refs[:inputs], *refs[inputs + earlier :])


def table_spec(place=lambda i: i):
    return pl.BlockSpec((ROWS, HD // 2), lambda m, i: (place(i), 0))


def rope_tables(rows, head_dim):
    half = head_dim // 2
    inverse = 1.0 / rope_base ** (np.arange(half, dtype=np.float32) * np.float32(2.0 / head_dim))
    angle = np.arange(rows, dtype=np.float32)[:, None] * inverse.astype(np.float32)[None, :]
    return jnp.asarray(np.cos(angle), f32), jnp.asarray(np.sin(angle), f32)


def attention_forward(core, tokens, weights, gains, tables, micro, earlier=()):
    micros, rows, width = tokens.shape
    blocks = rows // ROWS
    half = HEADS * HD // 2
    shapes = (
        struct((micros, rows, width), bf16),
        struct((micros, HEADS, rows, HD), f32),
        struct((micros, HEADS, rows, HD), bf16),
        struct((micros, rows, HD), f32),
        struct((micros, rows, HD), bf16),
        struct((micros, rows, HD), bf16),
        struct((micros, rows, half), bf16),
        struct((micros, rows, half), bf16),
        struct((micros, blocks, 8, HEADS * ROWS), f32),
    )
    heads = heads_spec(micro=micro)
    narrow = rows_spec(HD, micro=micro)
    specs = (rows_spec(width, micro=micro), heads, heads, narrow, narrow, narrow) + (
        rows_spec(half, micro=micro),
        rows_spec(half, micro=micro),
        stat_spec(micro=micro),
    )
    operands = (core, tokens, *weights, *gains, *tables)
    return pl.pallas_call(
        onward(attention_forward_kernel, len(operands), len(earlier)),
        grid=(1, blocks),
        in_specs=[pl.BlockSpec(memory_space=pltpu.SMEM), rows_spec(width, micro=micro)] + [whole(w) for w in weights] + [whole(g) for g in gains]
        + [table_spec()] * 2 + [pl.BlockSpec(memory_space=pl.ANY)] * len(earlier),
        out_specs=specs,
        out_shape=shapes,
        scratch_shapes=[pltpu.VMEM((rows, HD), bf16), pltpu.VMEM((rows, HD), bf16)],
        input_output_aliases={len(operands) + i: i for i in range(len(earlier))},
        compiler_params=params(60),
        cost_estimate=cost(5 * 10**9, 20 << 20),
        name="attention_forward",
    )(*operands, *earlier)


def ffn_spec(width):
    return pl.BlockSpec((1, FFN_ROWS, width), lambda m, i: (m, i, 0))


def feed_forward(lengths, tokens, cotangent, mixed, weights, gains):
    micros, rows, width = tokens.shape
    blocks = rows // ROWS
    hidden = weights[0].shape[1] // 2
    shapes = (
        struct((micros, rows, width), bf16),
        struct((micros, rows, width), f32),
        struct((micros, HEADS, rows, HD), bf16),
        struct((micros, blocks, 8, HEADS * ROWS), f32),
        struct((micros, rows, width), bf16),
        struct((micros, rows, width), bf16),
        struct((micros, rows, width), bf16),
    ) + (struct((micros, rows, hidden), bf16),) * 2 + (struct((micros, rows, 2 * hidden), bf16),) * 2 + (
        struct((8, width), f32),
    )
    specs = (
        ffn_spec(width), ffn_spec(width), pl.BlockSpec((1, HEADS, FFN_ROWS, HD), lambda m, i: (m, 0, i, 0)), pl.BlockSpec((1, FFN_ROWS // ROWS, 8, HEADS * ROWS), lambda m, i: (m, i, 0, 0)), ffn_spec(width), ffn_spec(width), ffn_spec(width),
    ) + (ffn_spec(hidden),) * 2 + (ffn_spec(2 * hidden),) * 2 + (
        pl.BlockSpec((8, width), lambda m, i: (0, 0)),
    )
    return pl.pallas_call(
        feed_forward_kernel,
        grid=(micros, rows // FFN_ROWS),
        in_specs=[pl.BlockSpec(memory_space=pltpu.SMEM), ffn_spec(width), ffn_spec(width)]
        + [ffn_spec(HEADS * HD // 2)] * 2
        + [whole(w) for w in weights]
        + [whole(g) for g in gains],
        out_specs=specs,
        out_shape=shapes,
        scratch_shapes=[pltpu.VMEM((FFN_ROWS, 2 * hidden), bf16), pltpu.VMEM((FFN_ROWS, 2 * hidden), bf16)],
        compiler_params=params(56),
        cost_estimate=cost(38 * 10**9, 80 << 20),
        name="feed_forward",
    )(lengths, tokens, cotangent, *mixed, *weights, *gains)


def attention_backward(core, saved, grads, tokens, weights, gains, tables, micro, earlier=()):
    _, qlin, qrot, klin, krot, value, _, _, lse = saved
    grad_hidden, grad_mixed, dots = grads
    micros, rows, width = tokens.shape
    blocks = rows // ROWS
    half = HEADS * HD // 2

    def early(i):
        return jnp.minimum(i, blocks - 1)

    def late(i):
        return jnp.maximum(i - 2, 0)

    keys = pl.BlockSpec((1, rows, HD), lambda m, i: (m + micro, 0, 0))
    shapes = (
        struct((micros, rows, width), bf16),
        struct((micros, rows, half + HD), bf16),
        struct((micros, rows, half + HD), bf16),
        struct((8, width), f32),
    )
    specs = tuple(rows_spec(size, late, micro) for size in (width, half + HD, half + HD)) + (
        pl.BlockSpec((8, width), lambda m, i: (0, 0)),
    )
    operands = (
        qrot, qlin, grad_mixed, lse, dots, *tables, krot, value, klin, *tables, tokens, grad_hidden, core, *weights, *gains,
    )
    return pl.pallas_call(
        onward(attention_backward_kernel, len(operands), len(earlier)),
        grid=(1, blocks + 2),
        in_specs=[heads_spec(early, micro)] * 3 + [stat_spec(early, micro)] * 2 + [table_spec(early)] * 2 + [keys] * 2
        + [rows_spec(HD, late, micro)] + [table_spec(late)] * 2 + [rows_spec(width, late, micro)] * 2
        + [pl.BlockSpec(memory_space=pltpu.SMEM)] + [whole(w) for w in weights] + [whole(g) for g in gains]
        + [pl.BlockSpec(memory_space=pl.ANY)] * len(earlier),
        out_specs=specs,
        out_shape=shapes,
        scratch_shapes=[pltpu.VMEM((rows, HD), f32), pltpu.VMEM((rows, HD), f32), pltpu.VMEM((rows, HEADS * HD), bf16)],
        input_output_aliases={len(operands) + i: i for i in range(len(earlier))},
        compiler_params=params(60),
        cost_estimate=cost(9 * 10**9, 20 << 20),
        name="attention_backward",
    )(*operands, *earlier)


def weight_grad(left, right):
    return dot_left(left.reshape(-1, left.shape[-1]), right.reshape(-1, right.shape[-1])).astype(bf16)


def fold(operands, groups, scalars, grid, outs):
    flat_terms = [term for group in groups for columns in group for term in columns]

    def kernel(_, *refs):
        sources, targets = refs[: len(flat_terms)], refs[len(flat_terms) :]
        at = 0
        for group, target in zip(groups, targets):
            start = 0
            for columns in group:
                value = sources[at][...].astype(f32)
                for more in range(1, len(columns)):
                    value = value + sources[at + more][...].astype(f32)
                width = value.shape[-1]
                target[..., start : start + width] = value.reshape(target.shape[:-1] + (width,)).astype(target.dtype)
                start += width
                at += len(columns)

    return pl.pallas_call(
        kernel,
        grid_spec=pltpu.PrefetchScalarGridSpec(
            num_scalar_prefetch=1,
            grid=grid,
            in_specs=[pl.BlockSpec(block, index) for _, block, index in flat_terms],
            out_specs=tuple(pl.BlockSpec(block, index) for _, block, index, _ in outs),
        ),
        out_shape=tuple(struct(shape, kind) for shape, _, _, kind in outs),
        compiler_params=pltpu.CompilerParams(vmem_limit_bytes=24 << 20, dimension_semantics=("arbitrary",)),
        cost_estimate=cost(10**6, 8 << 20),
        name="fold",
    )(scalars, *[operands[i] for i, _, _ in flat_terms])


def factors(count):
    side = 1
    while 2 * side**3 < count:
        side += 1
    return (2 * side, side, side) if 2 * side**3 == count else (count, 1, 1)


def place(sizes, axis):
    index = lax.axis_index("fsdp")
    for size in sizes[axis + 1 :]:
        index = index // size
    return index % sizes[axis]


def shifted(sizes, axis, step):
    stride = 1
    for size in sizes[axis + 1 :]:
        stride *= size
    pairs = []
    for index in range(sizes[0] * sizes[1] * sizes[2]):
        at = (index // stride) % sizes[axis]
        pairs.append((index, index + ((at + step) % sizes[axis] - at) * stride))
    return pairs


def tie(*trees):
    return lax.optimization_barrier(trees)


def ring_pairs(sizes, turn, step):
    pairs = []
    for core in range(2):
        axis = 1 if (core == 0) == (turn == 0) else 2
        pairs += [(2 * source + core, 2 * target + core) for source, target in shifted(sizes, axis, step)]
    return pairs


def place_at(sizes, turn, core):
    first, second = place(sizes, 1), place(sizes, 2)
    return jnp.where(core == 0, first, second) if turn == 0 else jnp.where(core == 0, second, first)


def sent_turn(block, sizes, turn):
    return [block] + [
        lax.ppermute(block, ("fsdp", "dp"), ring_pairs(sizes, turn, step)) for step in range(1, sizes[1])
    ]


def sent_z(block, sizes):
    return [block] + [lax.ppermute(block, "fsdp", shifted(sizes, 0, step)) for step in range(1, sizes[0])]


def joined_z(pieces, sizes):
    here, size = place(sizes, 0), sizes[0]
    rows = []
    for at in range(size):
        row = pieces[-1]
        for step in range(size - 1):
            row = jnp.where((here - at) % size == step, pieces[step], row)
        rows.append(row)
    return jnp.stack(rows)


def sent_middle(block, sizes, core):
    return sent_turn(block, sizes, 0)


def joined_middle(pieces, sizes, core):
    here, side = place_at(sizes, 0, core), sizes[1]
    if side == 1:
        return pieces[0][:, None]
    if side == 2:
        own, other = pieces
        return jnp.stack([jnp.where(here == 0, own, other), jnp.where(here == 0, other, own)], axis=1)
    out = jnp.zeros(pieces[0].shape[:1] + (side,) + pieces[0].shape[1:], pieces[0].dtype)
    for step, piece in enumerate(pieces):
        out = lax.dynamic_update_slice_in_dim(out, piece[:, None], (here - step) % side, 1)
    return out


def sent_last(block, sizes, core):
    return sent_turn(block, sizes, 1)


def joined_last(pieces, sizes, core):
    here, side = place_at(sizes, 1, core), sizes[1]
    if side == 2:
        own, other = pieces
        low = jnp.where(here == 0, own, other)
        high = jnp.where(here == 0, other, own)
        cross = [jnp.where(core == 0, high[:, 0], low[:, 1]), jnp.where(core == 0, low[:, 1], high[:, 0])]
        return jnp.stack([low[:, 0], cross[0], cross[1], high[:, 1]], axis=1)
    out = jnp.zeros(pieces[0].shape[:1] + (side * side,) + pieces[0].shape[2:], pieces[0].dtype)
    for step, piece in enumerate(pieces):
        there = (here - step) % side
        for k in range(side):
            at = jnp.where(core == 0, side * k + there, side * there + k)
            out = lax.dynamic_update_slice_in_dim(out, piece[:, k : k + 1], at, 1)
    return out


def gather_middle(block, sizes, core):
    return joined_middle(sent_middle(block, sizes, core), sizes, core)


def gather_last(block, sizes, core):
    return joined_last(sent_last(block, sizes, core), sizes, core)


def flat(block):
    return block.reshape(-1, block.shape[-1])


def swap(block):
    return lax.ppermute(block, "dp", [(0, 1), (1, 0)])


def total(parts):
    out = parts[0].astype(jnp.float32)
    for part in parts[1:]:
        out = out + part.astype(jnp.float32)
    return out


def boxed(mine, arrived, sizes):
    box = (sizes[0], sizes[1] * sizes[2], mine.shape[0] // (sizes[0] * sizes[1] * sizes[2]), mine.shape[1])
    return [mine.reshape(box)] + ([] if arrived is None else [arrived.reshape(box)])


def moved(sent, sizes, turn):
    return [
        lax.ppermute(piece, ("fsdp", "dp"), ring_pairs(sizes, turn, step)) for step, piece in enumerate(sent, 1)
    ]


def moved_z(sent, sizes):
    return [lax.ppermute(piece, "fsdp", shifted(sizes, 0, step)) for step, piece in enumerate(sent, 1)]


def fold_first(bundle, sizes, core):
    here, side = place_at(sizes, 1, core), sizes[1]
    places = []
    for step in range(side):
        there = (here + step) % side
        places += [jnp.where(core == 0, side * k + there, side * there + k) for k in range(side)]
    box = bundle[0][0].shape
    width = sum(parts[0].shape[-1] for parts in bundle)
    operands, groups, outs = [], [], []
    for step in range(side):
        group = []
        for parts in bundle:
            block = (box[0], 1, box[2], parts[0].shape[-1])
            columns = []
            for part in parts:
                operands.append(part)
                columns.append((len(operands) - 1, block, lambda k, at, step=step: (0, at[step * side + k], 0, 0)))
            group.append(columns)
        groups.append(group)
        outs.append(
            (
                (box[0], side, box[2], width),
                (box[0], 1, box[2], width),
                lambda k, at: (0, k, 0, 0),
                bf16 if step else f32,
            )
        )
    keep, *sent = fold(operands, groups, jnp.stack(places).astype(jnp.int32), (side,), outs)
    return keep, sent


def fold_middle(bundle, sizes, core):
    here, side = place_at(sizes, 0, core), sizes[1]
    box = bundle[0][0].shape
    width = sum(parts[0].shape[-1] for parts in bundle)
    operands, groups, outs = [], [], []
    for step in range(side):
        group = []
        for parts in bundle:
            block = (1, 1, box[2], parts[0].shape[-1])
            columns = []
            for part in parts:
                operands.append(part)
                columns.append((len(operands) - 1, block, lambda z, at, step=step: (z, at[step], 0, 0)))
            group.append(columns)
        groups.append(group)
        outs.append(
            ((box[0], box[2], width), (1, box[2], width), lambda z, at: (z, 0, 0), bf16 if step else f32)
        )
    places = jnp.stack([(here + step) % side for step in range(side)]).astype(jnp.int32)
    keep, *sent = fold(operands, groups, places, (box[0],), outs)
    return keep, sent


def fold_z(parts, sizes):
    here, size = place(sizes, 0), sizes[0]
    _, rows, width = parts[0].shape
    groups, outs = [], []
    for step in range(size):
        groups.append(
            [[(i, (1, rows, width), lambda z, at, step=step: (at[step], 0, 0)) for i in range(len(parts))]]
        )
        outs.append(((rows, width), (rows, width), lambda z, at: (0, 0), bf16 if step else f32))
    places = jnp.stack([(here + step) % size for step in range(size)]).astype(jnp.int32)
    keep, *sent = fold(parts, groups, places, (1,), outs)
    return keep, sent


def half_of(array, core, axis):
    size = array.shape[axis] // 2
    return lax.dynamic_slice_in_dim(array, core * size, size, axis)


def in_order(core, mine, theirs):
    return jnp.concatenate([jnp.where(core == 0, mine, theirs), jnp.where(core == 0, theirs, mine)], axis=1)


def pack_gains(pieces, rows):
    columns = [jnp.pad(piece, (0, rows - piece.shape[0])) for piece in pieces]
    return jnp.pad(jnp.stack(columns, axis=1), ((0, 0), (0, 128 - len(columns))))


def pack_gain_grads(pieces, count, rows):
    columns = [
        jnp.pad(piece.reshape(count, -1), ((0, 0), (0, rows - piece.shape[0] // count))).reshape(-1)
        for piece in pieces
    ]
    return jnp.pad(jnp.stack(columns, axis=1), ((0, 0), (0, 128 - len(columns))))


def local(
    sizes,
    tokens,
    cotangent,
    seq_lengths,
    slot_of,
    w_query,
    w_key,
    w_value,
    w_out,
    w_gate,
    w_up,
    w_down,
    gain_attn_in,
    gain_query,
    gain_key,
    gain_attn_out,
    gain_ffn_in,
    gain_ffn_out,
):
    micro_count = tokens.shape[0]
    count = lax.axis_size("fsdp")
    devices = count * lax.axis_size("dp")
    core = lax.axis_index("dp")
    device = lax.axis_index("fsdp") * lax.axis_size("dp") + core
    slots = jnp.arange(micro_count, dtype=jnp.int32) * devices + device
    lengths = jnp.sum(
        jnp.where(slot_of[None, :] == slots[:, None], seq_lengths[None, :], 0), axis=1
    )
    rows = w_query.shape[0]
    gains = (gain_attn_in, gain_query, gain_key, gain_attn_out, gain_ffn_in, gain_ffn_out)
    gain_rows = tuple(piece.shape[0] for piece in gains)

    half, hidden = HEADS * HD // 2, w_gate.shape[1] // 2
    first = jnp.concatenate(
        [half_of(w_query, core, 1), jnp.where(core == 0, w_key, w_value), pack_gains(gains, rows)], axis=1
    )
    wide = jnp.concatenate([half_of(w_gate, core, 1), half_of(w_up, core, 1)], axis=1)
    deep = jnp.concatenate([half_of(w_down, core, 0).T, half_of(w_out, core, 0).T], axis=1)
    first = sent_z(first, sizes)
    first, wide = tie(first, wide)
    wide = sent_z(wide, sizes)
    first = flat(gather_last(gather_middle(joined_z(first, sizes), sizes, core), sizes, core))
    first, wide = tie(first, wide)
    wide, deep = tie(wide, deep)
    deep = sent_z(deep, sizes)
    attn_weights = (first, swap(first))
    full_gains = [
        first[:, half + HD + i].reshape(count, rows)[:, :size].reshape(1, -1).astype(f32)
        for i, size in enumerate(gain_rows)
    ]
    tables = rope_tables(tokens.shape[1], HD)
    which = jnp.reshape(core, (1,)).astype(jnp.int32)
    wide = joined_z(wide, sizes)
    wide, attn_weights = tie(wide, attn_weights)
    wide = sent_middle(wide, sizes, core)
    saved = attention_forward(which, tokens, attn_weights, full_gains[:3], tables, 0)
    wide, deep, saved = tie(wide, deep, saved)
    wide, deep = joined_middle(wide, sizes, core), joined_z(deep, sizes)
    wide, deep, saved = tie(wide, deep, saved)
    deep, wide = sent_middle(deep, sizes, core), sent_last(wide, sizes, core)
    for micro in range(1, micro_count):
        saved = attention_forward(which, tokens, attn_weights, full_gains[:3], tables, micro, saved)
    deep, saved = tie(deep, saved)
    deep = joined_middle(deep, sizes, core)
    wide, deep = tie(wide, deep)
    deep = sent_last(deep, sizes, core)
    wide = flat(joined_last(wide, sizes, core))
    wide_swapped = swap(wide)
    deep = flat(joined_last(deep, sizes, core))
    ffn_weights = (wide, wide_swapped, deep, swap(deep))

    mixed = saved[6:8]
    (
        outputs, grad_hidden, grad_mixed, dots, ffn_in, grad_result, grad_att,
        inner_mine, inner_theirs, grad_mine, grad_theirs, gains_ffn,
    ) = feed_forward(lengths, tokens, cotangent, mixed, ffn_weights, full_gains[3:])
    wide = weight_grad(ffn_in, grad_theirs)
    wide, grad_mine = tie(wide, grad_mine)
    wide_arrived = swap(wide)
    wide = weight_grad(ffn_in, grad_mine)
    wide_keep, wide_sent = fold_first([boxed(wide, wide_arrived, sizes)], sizes, core)
    wide_sent, grad_mixed = tie(wide_sent, grad_mixed)
    wide_arrived = moved(wide_sent, sizes, 1)
    for micro in range(micro_count):
        *back, gains_own = attention_backward(
            which, saved, (grad_hidden, grad_mixed, dots), tokens, attn_weights, full_gains[:3], tables,
            micro, back if micro else (),
        )
        gains_attn = gains_attn + gains_own if micro else gains_own
        if micro == 0:
            wide_arrived, back, inner_theirs, grad_att = tie(wide_arrived, back, inner_theirs, grad_att)
            wide_keep, wide_sent = fold_middle([[wide_keep, *wide_arrived]], sizes, core)
            wide_sent, back, inner_theirs, grad_att = tie(wide_sent, back, inner_theirs, grad_att)
            wide_arrived = moved(wide_sent, sizes, 0)
            deep = [weight_grad(grad_result, inner_theirs), weight_grad(grad_att, mixed[1])]
            deep, inner_mine, grad_att = tie(deep, inner_mine, grad_att)
            deep_arrived = [swap(piece) for piece in deep]
            deep = [weight_grad(grad_result, inner_mine), weight_grad(grad_att, mixed[0])]
            deep = [boxed(own, piece, sizes) for own, piece in zip(deep, deep_arrived)]
            deep_keep, deep_sent = fold_first(deep, sizes, core)
            wide_arrived, deep_sent, back = tie(wide_arrived, deep_sent, back)
            wide_keep, wide_sent = fold_z([wide_keep, *wide_arrived], sizes)
            wide_sent, deep_sent, back = tie(wide_sent, deep_sent, back)
            deep_arrived, wide_arrived = moved(deep_sent, sizes, 1), moved_z(wide_sent, sizes)
    wide_arrived, deep_arrived, back = tie(wide_arrived, deep_arrived, back)
    deep_keep, deep_sent = fold_middle([[deep_keep, *deep_arrived]], sizes, core)
    deep_sent, back = tie(deep_sent, back)
    deep_arrived = moved(deep_sent, sizes, 0)
    input_grad, grad_mine, grad_theirs = back
    gain_grads = (
        gains_attn[0], gains_attn[1, :HD], gains_attn[2, :HD], gains_ffn[0], gains_ffn[1], gains_ffn[2],
    )
    gain_block = pack_gain_grads(gain_grads, count, rows).astype(bf16)
    normed = saved[0]
    d_theirs = weight_grad(normed, grad_theirs)
    d_theirs, grad_mine = tie(d_theirs, grad_mine)
    d_mine = weight_grad(normed, grad_mine)
    narrow = [boxed(d_mine, swap(d_theirs), sizes), boxed(gain_block, None, sizes)]
    narrow_keep, narrow_sent = fold_first(narrow, sizes, core)
    deep_arrived, narrow_sent = tie(deep_arrived, narrow_sent)
    deep_keep, deep_sent = fold_z([deep_keep, *deep_arrived], sizes)
    deep_sent, narrow_sent = tie(deep_sent, narrow_sent)
    narrow_arrived, deep_arrived = moved(narrow_sent, sizes, 1), moved_z(deep_sent, sizes)
    narrow_keep, narrow_sent = fold_middle([[narrow_keep, *narrow_arrived]], sizes, core)
    narrow_arrived = moved(narrow_sent, sizes, 0)
    deep_arrived, narrow_arrived = tie(deep_arrived, narrow_arrived)
    narrow_keep, narrow_sent = fold_z([narrow_keep, *narrow_arrived], sizes)
    narrow_arrived = moved_z(narrow_sent, sizes)
    early = jnp.concatenate([total([wide_keep, *wide_arrived]), total([deep_keep, *deep_arrived])], axis=1)
    early_theirs = swap(early)

    def shard(mine, theirs, start, width):
        return in_order(core, mine[:, start : start + width], theirs[:, start : start + width])

    starts = ((0, hidden), (hidden, hidden), (2 * hidden, hidden), (3 * hidden, half))
    shards = [shard(early, early_theirs, *place) for place in starts]
    shards, narrow_arrived = tie(shards, narrow_arrived)
    narrow = total([narrow_keep, *narrow_arrived])
    narrow_theirs = swap(narrow)
    keyval = shard(narrow, narrow_theirs, half, HD)
    gain_sums = narrow[:, half + HD :] + narrow_theirs[:, half + HD :]
    return (
        outputs,
        input_grad,
        shard(narrow, narrow_theirs, 0, half),
        keyval[:, :HD],
        keyval[:, HD:],
        shards[3].T,
        shards[0],
        shards[1],
        shards[2].T,
    ) + tuple(gain_sums[:size, i] for i, size in enumerate(gain_rows))


def solution(mesh):
    sizes = factors(mesh.shape["fsdp"])
    in_specs = (
        P(None, ("fsdp", "dp"), None),
        P(None, ("fsdp", "dp"), None),
        P(),
        P(),
        P("fsdp", None),
        P("fsdp", None),
        P("fsdp", None),
        P(None, "fsdp"),
        P("fsdp", None),
        P("fsdp", None),
        P(None, "fsdp"),
        P("fsdp"),
        P("fsdp"),
        P("fsdp"),
        P("fsdp"),
        P("fsdp"),
        P("fsdp"),
    )
    out_specs = (
        P(None, ("fsdp", "dp"), None),
        P(None, ("fsdp", "dp"), None),
        P("fsdp", None),
        P("fsdp", None),
        P("fsdp", None),
        P(None, "fsdp"),
        P("fsdp", None),
        P("fsdp", None),
        P(None, "fsdp"),
        P("fsdp"),
        P("fsdp"),
        P("fsdp"),
        P("fsdp"),
        P("fsdp"),
        P("fsdp"),
    )
    return jax.shard_map(functools.partial(local, sizes), mesh=mesh, in_specs=in_specs, out_specs=out_specs, check_vma=False)
```

```python
import functools

import jax
import jax.numpy as jnp
import numpy as np
from jax import lax
from jax.experimental import pallas as pl
from jax.experimental.pallas import tpu as pltpu
from jax.sharding import PartitionSpec as P

HEADS = 4
HD = 256
norm_eps = 1e-06
rope_base = 10000.0
ROWS = 256
FFN_ROWS = 512
CHUNK = 1024
LOG2E = 1.4426950408889634
f32 = jnp.float32
bf16 = jnp.bfloat16


def dot(left, right):
    return jnp.dot(left, right, preferred_element_type=f32)


def dot_right(left, right):
    return lax.dot_general(left, right, (((1,), (1,)), ((), ())), preferred_element_type=f32)


def dot_left(left, right):
    return lax.dot_general(left, right, (((0,), (0,)), ((), ())), preferred_element_type=f32)


def inverse_rms(value):
    return lax.rsqrt(jnp.mean(value * value, axis=-1, keepdims=True) + norm_eps)


def norm_back(value, gain, grad):
    scale = inverse_rms(value)
    unit = value * scale
    weighted = gain * grad
    inner = jnp.mean(unit * weighted, axis=-1, keepdims=True)
    return scale * (weighted - unit * inner), jnp.sum(unit * grad, axis=0, keepdims=True)


def rotate(value, cosine, sine):
    half = value.shape[-1] // 2
    first = value[:, :half]
    second = value[:, half:]
    return jnp.concatenate([first * cosine - second * sine, second * cosine + first * sine], axis=1)


def as_row(column):
    return jnp.transpose(jnp.broadcast_to(column, (column.shape[0], 128)))[:8]


def key_after_query(transposed):
    shape = (ROWS, ROWS)
    query = lax.broadcasted_iota(jnp.int32, shape, 1 if transposed else 0)
    key = lax.broadcasted_iota(jnp.int32, shape, 0 if transposed else 1)
    return key > query


def key_and_value(core, mine, theirs):
    half = HEADS * HD // 2
    left, right = mine[:, half : half + HD], theirs[:, half : half + HD]
    first = jnp.full(left.shape, core[0], jnp.int32) == 0
    return jnp.where(first, left, right), jnp.where(first, right, left)


def attention_forward_kernel(
    core, tok, mine, theirs, gain_in, gain_q, gain_k, cos, sin,
    a_out, qlin_out, qrot_out, klin_out, krot_out, v_out, mixed_mine, mixed_theirs, lse_out, k_all, v_all,
):
    block = pl.program_id(1)
    inputs = tok[0].astype(f32)
    normed = (inputs * inverse_rms(inputs) * gain_in[...]).astype(bf16)
    a_out[0] = normed
    cosine, sine = cos[...], sin[...]

    def prepared(linear, gain):
        return rotate(linear * inverse_rms(linear) * gain, cosine, sine).astype(bf16)

    here = pl.ds(pl.multiple_of(block * ROWS, ROWS), ROWS)
    wk, wv = key_and_value(core, mine, theirs)
    key_lin = dot(normed, wk)
    klin_out[0] = key_lin
    key_rot = prepared(key_lin, gain_k[...])
    krot_out[0] = key_rot
    k_all[here, :] = key_rot
    value = dot(normed, wv).astype(bf16)
    v_out[0] = value
    v_all[here, :] = value
    for half, weight in enumerate((mine, theirs)):
        linear = dot(normed, weight[:, : HEADS * HD // 2])
        for head in range(2):
            part = linear[:, head * HD : (head + 1) * HD]
            qlin_out[0, 2 * half + head] = part
            qrot_out[0, 2 * half + head] = prepared(part, gain_q[...])

    def attend(steps):
        queries = qrot_out[0].reshape(HEADS * ROWS, HD)
        after = key_after_query(False)[None]
        mass = jnp.zeros((HEADS * ROWS, 128), f32)
        mixed = jnp.zeros((HEADS * ROWS, HD), f32)
        for step in steps:
            keys = pl.ds(pl.multiple_of((block - step) * ROWS, ROWS), ROWS)
            expon = jnp.exp2(dot_right(queries, k_all[keys, :]) * (LOG2E * HD**-0.5))
            if step != 1:
                expon = expon.reshape(HEADS, ROWS, ROWS)
                keep = jnp.logical_not(after) if step == 0 else after
                expon = jnp.where(keep, expon, 0.0).reshape(HEADS * ROWS, ROWS)
            mass = mass + (expon[:, :128] + expon[:, 128:])
            mixed = mixed + dot(expon.astype(bf16), v_all[keys, :])
        sums = jnp.sum(mass, axis=-1, keepdims=True)
        mixed = (mixed * (1.0 / sums)).astype(bf16)
        for head in range(HEADS):
            mixed_out = (mixed_mine, mixed_theirs)[head // 2]
            columns = slice((head % 2) * HD, (head % 2 + 1) * HD)
            mixed_out[0, :, columns] = mixed[head * ROWS : (head + 1) * ROWS]
        lse_out[0, 0] = as_row(jnp.log(sums) * LOG2E)

    pl.when(block == 0)(lambda: attend((0,)))
    pl.when(block == 1)(lambda: attend((1, 0)))
    pl.when(block >= 2)(lambda: attend((2, 1, 0)))


def feed_forward_kernel(
    lengths, tok, cot, mixed_mine, mixed_theirs, wide_mine, wide_theirs, deep_mine, deep_theirs,
    gain_ao, gain_fi, gain_fo,
    act_out, gh_out, gm_out, dots_out, fin_out, gres_out, gatt_out,
    inner_mine, inner_theirs, grad_mine, grad_theirs, gains_out, left_s, right_s,
):
    micro, block = pl.program_id(0), pl.program_id(1)
    half_width = wide_mine.shape[1] // 2
    rate, cubic = 0.7978845608028654, 0.044715
    gains = []

    def chain(part):
        here = slice(part * ROWS, (part + 1) * ROWS)
        inputs = tok[0, here].astype(f32)
        place = (block * FFN_ROWS + part * ROWS) + lax.broadcasted_iota(jnp.int32, (ROWS, 1), 0)
        valid = (place < lengths[micro]).astype(f32)
        attended = dot_right(mixed_mine[0, here], deep_mine[:, half_width:]) + dot_right(
            mixed_theirs[0, here], deep_theirs[:, half_width:]
        )
        yield
        hidden = inputs + attended * inverse_rms(attended) * gain_ao[...]
        ffn_in = (hidden * inverse_rms(hidden) * gain_fi[...]).astype(bf16)
        fin_out[0, here] = ffn_in
        result = jnp.zeros(inputs.shape, f32)
        for half in range(2):
            wide = (wide_mine, wide_theirs)[half]
            deep = (deep_mine, deep_theirs)[half]
            inner_out = (inner_mine, inner_theirs)[half]
            for start in range(0, half_width, CHUNK):
                yield
                columns = slice(start, start + CHUNK)
                shifted_columns = slice(half_width + start, half_width + start + CHUNK)
                kept = slice(half * half_width + start, half * half_width + start + CHUNK)
                gate = dot(ffn_in, wide[:, columns])
                up = dot(ffn_in, wide[:, shifted_columns])
                square = gate * gate
                tanh = jnp.tanh(gate * (rate + (rate * cubic) * square))
                side = 0.5 + 0.5 * tanh
                gelu = gate * side
                slope = side + gelu * (1.0 - tanh) * (rate + (3.0 * rate * cubic) * square)
                inner = (gelu * up).astype(bf16)
                inner_out[0, here, columns] = inner
                left_s[here, kept] = (up * slope).astype(bf16)
                right_s[here, kept] = gelu.astype(bf16)
                result = result + dot_right(inner, deep[:, columns])
        yield
        act_out[0, here] = (valid * (hidden + result * inverse_rms(result) * gain_fo[...])).astype(bf16)
        upstream = valid * cot[0, here].astype(f32)
        grad_result, g_fo = norm_back(result, gain_fo[...], upstream)
        grad_result = grad_result.astype(bf16)
        gres_out[0, here] = grad_result
        grad_in = jnp.zeros(inputs.shape, f32)
        for half in range(2):
            wide = (wide_mine, wide_theirs)[half]
            deep = (deep_mine, deep_theirs)[half]
            grad_out = (grad_mine, grad_theirs)[half]
            for start in range(0, half_width, CHUNK):
                yield
                columns = slice(start, start + CHUNK)
                shifted_columns = slice(half_width + start, half_width + start + CHUNK)
                kept = slice(half * half_width + start, half * half_width + start + CHUNK)
                grad_inner = dot(grad_result, deep[:, columns])
                grad_gate = (grad_inner * left_s[here, kept].astype(f32)).astype(bf16)
                grad_up = (grad_inner * right_s[here, kept].astype(f32)).astype(bf16)
                grad_out[0, here, columns] = grad_gate
                grad_out[0, here, shifted_columns] = grad_up
                grad_in = grad_in + dot_right(grad_gate, wide[:, columns])
                grad_in = grad_in + dot_right(grad_up, wide[:, shifted_columns])
        yield
        grad_hidden, g_fi = norm_back(hidden, gain_fi[...], grad_in)
        grad_hidden = upstream + grad_hidden
        gh_out[0, here] = grad_hidden
        grad_att, g_ao = norm_back(attended, gain_ao[...], grad_hidden)
        grad_att = grad_att.astype(bf16)
        gatt_out[0, here] = grad_att
        gains.append((g_ao, g_fi, g_fo))
        yield
        for head in range(HEADS):
            weight, mixed = ((deep_mine, mixed_mine), (deep_theirs, mixed_theirs))[head // 2]
            columns = slice((head % 2) * HD, (head % 2 + 1) * HD)
            out_columns = slice(half_width + columns.start, half_width + columns.stop)
            grad_mixed = dot(grad_att, weight[:, out_columns]).astype(bf16)
            gm_out[0, head, here] = grad_mixed
            product = jnp.sum(grad_mixed.astype(f32) * mixed[0, here, columns].astype(f32), axis=-1, keepdims=True)
            dots_out[0, part, :, head * ROWS : (head + 1) * ROWS] = as_row(product)
        yield

    chains = [chain(part) for part in range(FFN_ROWS // ROWS)]
    next(chains[0])
    for _ in range(5 + 4 * half_width // CHUNK):
        for one in reversed(chains):
            next(one, None)
    for one in chains:
        for _ in one:
            pass

    @pl.when((micro == 0) & (block == 0))
    def _():
        gains_out[...] = jnp.zeros(gains_out.shape, f32)

    for own in gains:
        for row, piece in enumerate(own):
            gains_out[row : row + 1, :] += piece


def attention_backward_kernel(
    qrot, qlin, gm, lse, dots, cos, sin, krot, val, klin, cos_late, sin_late, tok, gh,
    core, mine, theirs, gain_in, gain_q, gain_k,
    input_out, grad_mine, grad_theirs, gains_out, dk, dv, gq_all,
):
    micro, step = pl.program_id(0), pl.program_id(1)

    @pl.when((micro == 0) & (step == 0))
    def _():
        gains_out[...] = jnp.zeros(gains_out.shape, f32)

    def unrotated(grad, cosine, sine):
        return rotate(grad * HD**-0.5, cosine, -sine)

    def attend(backs):
        queries = qrot[0].reshape(HEADS * ROWS, HD)
        grads = gm[0].reshape(HEADS * ROWS, HD)
        after = key_after_query(True)
        after = jnp.concatenate([after] * HEADS, axis=1)
        log_mass, row_dot = lse[0, 0, 0:1], dots[0, 0, 0:1]
        grad_queries = jnp.zeros((HEADS * ROWS, HD), f32)
        for back in backs:
            keys = pl.ds(pl.multiple_of((step - back) * ROWS, ROWS), ROWS)
            key, value = krot[0, keys, :], val[0, keys, :]
            probs = jnp.exp2(dot_right(key, queries) * (LOG2E * HD**-0.5) - log_mass)
            if back != 1:
                probs = jnp.where(jnp.logical_not(after) if back == 0 else after, probs, 0.0)
            grad_probs = dot_right(value, grads)
            grad_scores = (probs * (grad_probs - row_dot)).astype(bf16)
            grad_value = dot(probs.astype(bf16), grads)
            grad_key = dot(grad_scores, queries)
            if back == 0:
                dv[keys, :] = grad_value
                dk[keys, :] = grad_key
            else:
                dv[keys, :] += grad_value
                dk[keys, :] += grad_key
            grad_queries = grad_queries + dot_left(grad_scores, key)
        here = pl.ds(pl.multiple_of(step * ROWS, ROWS), ROWS)
        for head in range(HEADS):
            turned = unrotated(grad_queries[head * ROWS : (head + 1) * ROWS], cos[...], sin[...])
            grad_lin, g_q = norm_back(qlin[0, head], gain_q[...], turned)
            gq_all[here, head * HD : (head + 1) * HD] = grad_lin.astype(bf16)
            gains_out[1:2, :HD] += g_q

    pl.when(step == 0)(lambda: attend((0,)))
    pl.when(step == 1)(lambda: attend((1, 0)))
    pl.when((step == 2) | (step == 3))(lambda: attend((2, 1, 0)))

    @pl.when(step >= 2)
    def _():
        here = pl.ds(pl.multiple_of((step - 2) * ROWS, ROWS), ROWS)
        turned = unrotated(dk[here, :], cos_late[...], sin_late[...])
        grad_key, g_k = norm_back(klin[0], gain_k[...], turned)
        grad_key = grad_key.astype(bf16)
        grad_value = dv[here, :].astype(bf16)
        half = HEADS * HD // 2
        first, second = gq_all[here, :half], gq_all[here, half:]
        grad_mine[0, :, :half] = first
        grad_theirs[0, :, :half] = second
        is_first = jnp.full(grad_key.shape, core[0], jnp.int32) == 0
        grad_mine[0, :, half:] = jnp.where(is_first, grad_key, grad_value)
        grad_theirs[0, :, half:] = jnp.where(is_first, grad_value, grad_key)
        wk, wv = key_and_value(core, mine, theirs)
        grad_in = (
            dot_right(first, mine[:, :half])
            + dot_right(second, theirs[:, :half])
            + dot_right(grad_key, wk)
            + dot_right(grad_value, wv)
        )
        grad_inputs, g_in = norm_back(tok[0].astype(f32), gain_in[...], grad_in)
        input_out[0] = (gh[0] + grad_inputs).astype(bf16)
        gains_out[0:1, :] += g_in
        gains_out[2:3, :HD] += g_k


def whole(array):
    return pl.BlockSpec(array.shape, lambda m, i: (0,) * array.ndim, pipeline_mode=pl.Buffered(1))


def struct(shape, dtype):
    return jax.ShapeDtypeStruct(shape, dtype)


def params(limit):
    return pltpu.CompilerParams(vmem_limit_bytes=limit << 20, dimension_semantics=("arbitrary", "arbitrary"))


def cost(flops, size):
    return pl.CostEstimate(flops=flops, bytes_accessed=size, transcendentals=0)


def rows_spec(width, place=lambda i: i, micro=0):
    return pl.BlockSpec((1, ROWS, width), lambda m, i: (m + micro, place(i), 0))


def heads_spec(place=lambda i: i, micro=0):
    return pl.BlockSpec((1, HEADS, ROWS, HD), lambda m, i: (m + micro, 0, place(i), 0))


def stat_spec(place=lambda i: i, micro=0):
    return pl.BlockSpec((1, 1, 8, HEADS * ROWS), lambda m, i: (m + micro, place(i), 0, 0))


def onward(kernel, inputs, earlier):
    return lambda *refs: kernel(*refs[:inputs], *refs[inputs + earlier :])


def table_spec(place=lambda i: i):
    return pl.BlockSpec((ROWS, HD // 2), lambda m, i: (place(i), 0))


def rope_tables(rows, head_dim):
    half = head_dim // 2
    inverse = 1.0 / rope_base ** (np.arange(half, dtype=np.float32) * np.float32(2.0 / head_dim))
    angle = np.arange(rows, dtype=np.float32)[:, None] * inverse.astype(np.float32)[None, :]
    return jnp.asarray(np.cos(angle), f32), jnp.asarray(np.sin(angle), f32)


def attention_forward(core, tokens, weights, gains, tables, micro, earlier=()):
    micros, rows, width = tokens.shape
    blocks = rows // ROWS
    half = HEADS * HD // 2
    shapes = (
        struct((micros, rows, width), bf16),
        struct((micros, HEADS, rows, HD), f32),
        struct((micros, HEADS, rows, HD), bf16),
        struct((micros, rows, HD), f32),
        struct((micros, rows, HD), bf16),
        struct((micros, rows, HD), bf16),
        struct((micros, rows, half), bf16),
        struct((micros, rows, half), bf16),
        struct((micros, blocks, 8, HEADS * ROWS), f32),
    )
    heads = heads_spec(micro=micro)
    narrow = rows_spec(HD, micro=micro)
    specs = (rows_spec(width, micro=micro), heads, heads, narrow, narrow, narrow) + (
        rows_spec(half, micro=micro),
        rows_spec(half, micro=micro),
        stat_spec(micro=micro),
    )
    operands = (core, tokens, *weights, *gains, *tables)
    return pl.pallas_call(
        onward(attention_forward_kernel, len(operands), len(earlier)),
        grid=(1, blocks),
        in_specs=[pl.BlockSpec(memory_space=pltpu.SMEM), rows_spec(width, micro=micro)] + [whole(w) for w in weights] + [whole(g) for g in gains]
        + [table_spec()] * 2 + [pl.BlockSpec(memory_space=pl.ANY)] * len(earlier),
        out_specs=specs,
        out_shape=shapes,
        scratch_shapes=[pltpu.VMEM((rows, HD), bf16), pltpu.VMEM((rows, HD), bf16)],
        input_output_aliases={len(operands) + i: i for i in range(len(earlier))},
        compiler_params=params(60),
        cost_estimate=cost(5 * 10**9, 20 << 20),
        name="attention_forward",
    )(*operands, *earlier)


def ffn_spec(width):
    return pl.BlockSpec((1, FFN_ROWS, width), lambda m, i: (m, i, 0))


def feed_forward(lengths, tokens, cotangent, mixed, weights, gains):
    micros, rows, width = tokens.shape
    blocks = rows // ROWS
    hidden = weights[0].shape[1] // 2
    shapes = (
        struct((micros, rows, width), bf16),
        struct((micros, rows, width), f32),
        struct((micros, HEADS, rows, HD), bf16),
        struct((micros, blocks, 8, HEADS * ROWS), f32),
        struct((micros, rows, width), bf16),
        struct((micros, rows, width), bf16),
        struct((micros, rows, width), bf16),
    ) + (struct((micros, rows, hidden), bf16),) * 2 + (struct((micros, rows, 2 * hidden), bf16),) * 2 + (
        struct((8, width), f32),
    )
    specs = (
        ffn_spec(width), ffn_spec(width), pl.BlockSpec((1, HEADS, FFN_ROWS, HD), lambda m, i: (m, 0, i, 0)), pl.BlockSpec((1, FFN_ROWS // ROWS, 8, HEADS * ROWS), lambda m, i: (m, i, 0, 0)), ffn_spec(width), ffn_spec(width), ffn_spec(width),
    ) + (ffn_spec(hidden),) * 2 + (ffn_spec(2 * hidden),) * 2 + (
        pl.BlockSpec((8, width), lambda m, i: (0, 0)),
    )
    return pl.pallas_call(
        feed_forward_kernel,
        grid=(micros, rows // FFN_ROWS),
        in_specs=[pl.BlockSpec(memory_space=pltpu.SMEM), ffn_spec(width), ffn_spec(width)]
        + [ffn_spec(HEADS * HD // 2)] * 2
        + [whole(w) for w in weights]
        + [whole(g) for g in gains],
        out_specs=specs,
        out_shape=shapes,
        scratch_shapes=[pltpu.VMEM((FFN_ROWS, 2 * hidden), bf16), pltpu.VMEM((FFN_ROWS, 2 * hidden), bf16)],
        compiler_params=params(56),
        cost_estimate=cost(38 * 10**9, 80 << 20),
        name="feed_forward",
    )(lengths, tokens, cotangent, *mixed, *weights, *gains)


def attention_backward(core, saved, grads, tokens, weights, gains, tables, micro, earlier=()):
    _, qlin, qrot, klin, krot, value, _, _, lse = saved
    grad_hidden, grad_mixed, dots = grads
    micros, rows, width = tokens.shape
    blocks = rows // ROWS
    half = HEADS * HD // 2

    def early(i):
        return jnp.minimum(i, blocks - 1)

    def late(i):
        return jnp.maximum(i - 2, 0)

    keys = pl.BlockSpec((1, rows, HD), lambda m, i: (m + micro, 0, 0))
    shapes = (
        struct((micros, rows, width), bf16),
        struct((micros, rows, half + HD), bf16),
        struct((micros, rows, half + HD), bf16),
        struct((8, width), f32),
    )
    specs = tuple(rows_spec(size, late, micro) for size in (width, half + HD, half + HD)) + (
        pl.BlockSpec((8, width), lambda m, i: (0, 0)),
    )
    operands = (
        qrot, qlin, grad_mixed, lse, dots, *tables, krot, value, klin, *tables, tokens, grad_hidden, core, *weights, *gains,
    )
    return pl.pallas_call(
        onward(attention_backward_kernel, len(operands), len(earlier)),
        grid=(1, blocks + 2),
        in_specs=[heads_spec(early, micro)] * 3 + [stat_spec(early, micro)] * 2 + [table_spec(early)] * 2 + [keys] * 2
        + [rows_spec(HD, late, micro)] + [table_spec(late)] * 2 + [rows_spec(width, late, micro)] * 2
        + [pl.BlockSpec(memory_space=pltpu.SMEM)] + [whole(w) for w in weights] + [whole(g) for g in gains]
        + [pl.BlockSpec(memory_space=pl.ANY)] * len(earlier),
        out_specs=specs,
        out_shape=shapes,
        scratch_shapes=[pltpu.VMEM((rows, HD), f32), pltpu.VMEM((rows, HD), f32), pltpu.VMEM((rows, HEADS * HD), bf16)],
        input_output_aliases={len(operands) + i: i for i in range(len(earlier))},
        compiler_params=params(60),
        cost_estimate=cost(9 * 10**9, 20 << 20),
        name="attention_backward",
    )(*operands, *earlier)


def weight_grad(left, right):
    return dot_left(left.reshape(-1, left.shape[-1]), right.reshape(-1, right.shape[-1])).astype(bf16)


def fold(operands, groups, scalars, grid, outs):
    flat_terms = [term for group in groups for columns in group for term in columns]

    def kernel(_, *refs):
        sources, targets = refs[: len(flat_terms)], refs[len(flat_terms) :]
        at = 0
        for group, target in zip(groups, targets):
            start = 0
            for columns in group:
                value = sources[at][...].astype(f32)
                for more in range(1, len(columns)):
                    value = value + sources[at + more][...].astype(f32)
                width = value.shape[-1]
                target[..., start : start + width] = value.reshape(target.shape[:-1] + (width,)).astype(target.dtype)
                start += width
                at += len(columns)

    return pl.pallas_call(
        kernel,
        grid_spec=pltpu.PrefetchScalarGridSpec(
            num_scalar_prefetch=1,
            grid=grid,
            in_specs=[pl.BlockSpec(block, index) for _, block, index in flat_terms],
            out_specs=tuple(pl.BlockSpec(block, index) for _, block, index, _ in outs),
        ),
        out_shape=tuple(struct(shape, kind) for shape, _, _, kind in outs),
        compiler_params=pltpu.CompilerParams(vmem_limit_bytes=24 << 20, dimension_semantics=("arbitrary",)),
        cost_estimate=cost(10**6, 8 << 20),
        name="fold",
    )(scalars, *[operands[i] for i, _, _ in flat_terms])


def factors(count):
    side = 1
    while 2 * side**3 < count:
        side += 1
    return (2 * side, side, side) if 2 * side**3 == count else (count, 1, 1)


def place(sizes, axis):
    index = lax.axis_index("fsdp")
    for size in sizes[axis + 1 :]:
        index = index // size
    return index % sizes[axis]


def shifted(sizes, axis, step):
    stride = 1
    for size in sizes[axis + 1 :]:
        stride *= size
    pairs = []
    for index in range(sizes[0] * sizes[1] * sizes[2]):
        at = (index // stride) % sizes[axis]
        pairs.append((index, index + ((at + step) % sizes[axis] - at) * stride))
    return pairs


def tie(*trees):
    return lax.optimization_barrier(trees)


def ring_pairs(sizes, turn, step):
    pairs = []
    for core in range(2):
        axis = 1 if (core == 0) == (turn == 0) else 2
        pairs += [(2 * source + core, 2 * target + core) for source, target in shifted(sizes, axis, step)]
    return pairs


def place_at(sizes, turn, core):
    first, second = place(sizes, 1), place(sizes, 2)
    return jnp.where(core == 0, first, second) if turn == 0 else jnp.where(core == 0, second, first)


def sent_turn(block, sizes, turn):
    return [block] + [
        lax.ppermute(block, ("fsdp", "dp"), ring_pairs(sizes, turn, step)) for step in range(1, sizes[1])
    ]


def sent_z(block, sizes):
    return [block] + [lax.ppermute(block, "fsdp", shifted(sizes, 0, step)) for step in range(1, sizes[0])]


def joined_z(pieces, sizes):
    here, size = place(sizes, 0), sizes[0]
    rows = []
    for at in range(size):
        row = pieces[-1]
        for step in range(size - 1):
            row = jnp.where((here - at) % size == step, pieces[step], row)
        rows.append(row)
    return jnp.stack(rows)


def sent_middle(block, sizes, core):
    return sent_turn(block, sizes, 0)


def joined_middle(pieces, sizes, core):
    here, side = place_at(sizes, 0, core), sizes[1]
    if side == 1:
        return pieces[0][:, None]
    if side == 2:
        own, other = pieces
        return jnp.stack([jnp.where(here == 0, own, other), jnp.where(here == 0, other, own)], axis=1)
    out = jnp.zeros(pieces[0].shape[:1] + (side,) + pieces[0].shape[1:], pieces[0].dtype)
    for step, piece in enumerate(pieces):
        out = lax.dynamic_update_slice_in_dim(out, piece[:, None], (here - step) % side, 1)
    return out


def sent_last(block, sizes, core):
    return sent_turn(block, sizes, 1)


def joined_last(pieces, sizes, core):
    here, side = place_at(sizes, 1, core), sizes[1]
    if side == 2:
        own, other = pieces
        low = jnp.where(here == 0, own, other)
        high = jnp.where(here == 0, other, own)
        cross = [jnp.where(core == 0, high[:, 0], low[:, 1]), jnp.where(core == 0, low[:, 1], high[:, 0])]
        return jnp.stack([low[:, 0], cross[0], cross[1], high[:, 1]], axis=1)
    out = jnp.zeros(pieces[0].shape[:1] + (side * side,) + pieces[0].shape[2:], pieces[0].dtype)
    for step, piece in enumerate(pieces):
        there = (here - step) % side
        for k in range(side):
            at = jnp.where(core == 0, side * k + there, side * there + k)
            out = lax.dynamic_update_slice_in_dim(out, piece[:, k : k + 1], at, 1)
    return out


def gather_middle(block, sizes, core):
    return joined_middle(sent_middle(block, sizes, core), sizes, core)


def gather_last(block, sizes, core):
    return joined_last(sent_last(block, sizes, core), sizes, core)


def flat(block):
    return block.reshape(-1, block.shape[-1])


def swap(block):
    return lax.ppermute(block, "dp", [(0, 1), (1, 0)])


def total(parts):
    out = parts[0].astype(jnp.float32)
    for part in parts[1:]:
        out = out + part.astype(jnp.float32)
    return out


def boxed(mine, arrived, sizes):
    box = (sizes[0], sizes[1] * sizes[2], mine.shape[0] // (sizes[0] * sizes[1] * sizes[2]), mine.shape[1])
    return [mine.reshape(box)] + ([] if arrived is None else [arrived.reshape(box)])


def moved(sent, sizes, turn):
    return [
        lax.ppermute(piece, ("fsdp", "dp"), ring_pairs(sizes, turn, step)) for step, piece in enumerate(sent, 1)
    ]


def moved_z(sent, sizes):
    return [lax.ppermute(piece, "fsdp", shifted(sizes, 0, step)) for step, piece in enumerate(sent, 1)]


def fold_first(bundle, sizes, core):
    here, side = place_at(sizes, 1, core), sizes[1]
    places = []
    for step in range(side):
        there = (here + step) % side
        places += [jnp.where(core == 0, side * k + there, side * there + k) for k in range(side)]
    box = bundle[0][0].shape
    width = sum(parts[0].shape[-1] for parts in bundle)
    operands, groups, outs = [], [], []
    for step in range(side):
        group = []
        for parts in bundle:
            block = (box[0], 1, box[2], parts[0].shape[-1])
            columns = []
            for part in parts:
                operands.append(part)
                columns.append((len(operands) - 1, block, lambda k, at, step=step: (0, at[step * side + k], 0, 0)))
            group.append(columns)
        groups.append(group)
        outs.append(
            (
                (box[0], side, box[2], width),
                (box[0], 1, box[2], width),
                lambda k, at: (0, k, 0, 0),
                bf16 if step else f32,
            )
        )
    keep, *sent = fold(operands, groups, jnp.stack(places).astype(jnp.int32), (side,), outs)
    return keep, sent


def fold_middle(bundle, sizes, core):
    here, side = place_at(sizes, 0, core), sizes[1]
    box = bundle[0][0].shape
    width = sum(parts[0].shape[-1] for parts in bundle)
    operands, groups, outs = [], [], []
    for step in range(side):
        group = []
        for parts in bundle:
            block = (1, 1, box[2], parts[0].shape[-1])
            columns = []
            for part in parts:
                operands.append(part)
                columns.append((len(operands) - 1, block, lambda z, at, step=step: (z, at[step], 0, 0)))
            group.append(columns)
        groups.append(group)
        outs.append(
            ((box[0], box[2], width), (1, box[2], width), lambda z, at: (z, 0, 0), bf16 if step else f32)
        )
    places = jnp.stack([(here + step) % side for step in range(side)]).astype(jnp.int32)
    keep, *sent = fold(operands, groups, places, (box[0],), outs)
    return keep, sent


def fold_z(parts, sizes):
    here, size = place(sizes, 0), sizes[0]
    _, rows, width = parts[0].shape
    groups, outs = [], []
    for step in range(size):
        groups.append(
            [[(i, (1, rows, width), lambda z, at, step=step: (at[step], 0, 0)) for i in range(len(parts))]]
        )
        outs.append(((rows, width), (rows, width), lambda z, at: (0, 0), bf16 if step else f32))
    places = jnp.stack([(here + step) % size for step in range(size)]).astype(jnp.int32)
    keep, *sent = fold(parts, groups, places, (1,), outs)
    return keep, sent


def half_of(array, core, axis):
    size = array.shape[axis] // 2
    return lax.dynamic_slice_in_dim(array, core * size, size, axis)


def in_order(core, mine, theirs):
    return jnp.concatenate([jnp.where(core == 0, mine, theirs), jnp.where(core == 0, theirs, mine)], axis=1)


def pack_gains(pieces, rows):
    columns = [jnp.pad(piece, (0, rows - piece.shape[0])) for piece in pieces]
    return jnp.pad(jnp.stack(columns, axis=1), ((0, 0), (0, 128 - len(columns))))


def pack_gain_grads(pieces, count, rows):
    columns = [
        jnp.pad(piece.reshape(count, -1), ((0, 0), (0, rows - piece.shape[0] // count))).reshape(-1)
        for piece in pieces
    ]
    return jnp.pad(jnp.stack(columns, axis=1), ((0, 0), (0, 128 - len(columns))))


def local(
    sizes,
    tokens,
    cotangent,
    seq_lengths,
    slot_of,
    w_query,
    w_key,
    w_value,
    w_out,
    w_gate,
    w_up,
    w_down,
    gain_attn_in,
    gain_query,
    gain_key,
    gain_attn_out,
    gain_ffn_in,
    gain_ffn_out,
):
    micro_count = tokens.shape[0]
    count = lax.axis_size("fsdp")
    devices = count * lax.axis_size("dp")
    core = lax.axis_index("dp")
    device = lax.axis_index("fsdp") * lax.axis_size("dp") + core
    slots = jnp.arange(micro_count, dtype=jnp.int32) * devices + device
    lengths = jnp.sum(
        jnp.where(slot_of[None, :] == slots[:, None], seq_lengths[None, :], 0), axis=1
    )
    rows = w_query.shape[0]
    gains = (gain_attn_in, gain_query, gain_key, gain_attn_out, gain_ffn_in, gain_ffn_out)
    gain_rows = tuple(piece.shape[0] for piece in gains)

    half, hidden = HEADS * HD // 2, w_gate.shape[1] // 2
    first = jnp.concatenate(
        [half_of(w_query, core, 1), jnp.where(core == 0, w_key, w_value), pack_gains(gains, rows)], axis=1
    )
    wide = jnp.concatenate([half_of(w_gate, core, 1), half_of(w_up, core, 1)], axis=1)
    deep = jnp.concatenate([half_of(w_down, core, 0).T, half_of(w_out, core, 0).T], axis=1)
    first = sent_z(first, sizes)
    first, wide = tie(first, wide)
    wide = sent_z(wide, sizes)
    first = flat(gather_last(gather_middle(joined_z(first, sizes), sizes, core), sizes, core))
    first, wide = tie(first, wide)
    wide, deep = tie(wide, deep)
    deep = sent_z(deep, sizes)
    attn_weights = (first, swap(first))
    full_gains = [
        first[:, half + HD + i].reshape(count, rows)[:, :size].reshape(1, -1).astype(f32)
        for i, size in enumerate(gain_rows)
    ]
    tables = rope_tables(tokens.shape[1], HD)
    which = jnp.reshape(core, (1,)).astype(jnp.int32)
    wide = sent_middle(joined_z(wide, sizes), sizes, core)
    wide, attn_weights = tie(wide, attn_weights)
    wide = joined_middle(wide, sizes, core)
    wide, attn_weights = tie(wide, attn_weights)
    wide = sent_last(wide, sizes, core)
    saved = attention_forward(which, tokens, attn_weights, full_gains[:3], tables, 0)
    wide, deep, saved = tie(wide, deep, saved)
    deep = joined_z(deep, sizes)
    deep, saved = tie(deep, saved)
    deep = sent_middle(deep, sizes, core)
    for micro in range(1, micro_count):
        saved = attention_forward(which, tokens, attn_weights, full_gains[:3], tables, micro, saved)
    deep, saved = tie(deep, saved)
    deep = joined_middle(deep, sizes, core)
    wide, deep = tie(wide, deep)
    deep = sent_last(deep, sizes, core)
    wide = flat(joined_last(wide, sizes, core))
    wide_swapped = swap(wide)
    deep = flat(joined_last(deep, sizes, core))
    ffn_weights = (wide, wide_swapped, deep, swap(deep))

    mixed = saved[6:8]
    (
        outputs, grad_hidden, grad_mixed, dots, ffn_in, grad_result, grad_att,
        inner_mine, inner_theirs, grad_mine, grad_theirs, gains_ffn,
    ) = feed_forward(lengths, tokens, cotangent, mixed, ffn_weights, full_gains[3:])
    wide = weight_grad(ffn_in, grad_theirs)
    wide, grad_mine = tie(wide, grad_mine)
    wide_arrived = swap(wide)
    wide = weight_grad(ffn_in, grad_mine)
    wide_keep, wide_sent = fold_first([boxed(wide, wide_arrived, sizes)], sizes, core)
    wide_sent, grad_mixed = tie(wide_sent, grad_mixed)
    wide_arrived = moved(wide_sent, sizes, 1)
    for micro in range(micro_count):
        *back, gains_own = attention_backward(
            which, saved, (grad_hidden, grad_mixed, dots), tokens, attn_weights, full_gains[:3], tables,
            micro, back if micro else (),
        )
        gains_attn = gains_attn + gains_own if micro else gains_own
        if micro == 0:
            wide_arrived, back, inner_theirs, grad_att = tie(wide_arrived, back, inner_theirs, grad_att)
            wide_keep, wide_sent = fold_middle([[wide_keep, *wide_arrived]], sizes, core)
            wide_sent, back, inner_theirs, grad_att = tie(wide_sent, back, inner_theirs, grad_att)
            wide_arrived = moved(wide_sent, sizes, 0)
            deep = [weight_grad(grad_result, inner_theirs), weight_grad(grad_att, mixed[1])]
            deep, inner_mine, grad_att = tie(deep, inner_mine, grad_att)
            deep_arrived = [swap(piece) for piece in deep]
            deep = [weight_grad(grad_result, inner_mine), weight_grad(grad_att, mixed[0])]
            deep = [boxed(own, piece, sizes) for own, piece in zip(deep, deep_arrived)]
            deep_keep, deep_sent = fold_first(deep, sizes, core)
            wide_arrived, deep_sent, back = tie(wide_arrived, deep_sent, back)
            wide_keep, wide_sent = fold_z([wide_keep, *wide_arrived], sizes)
            wide_sent, deep_sent, back = tie(wide_sent, deep_sent, back)
            deep_arrived, wide_arrived = moved(deep_sent, sizes, 1), moved_z(wide_sent, sizes)
    wide_arrived, deep_arrived, back = tie(wide_arrived, deep_arrived, back)
    deep_keep, deep_sent = fold_middle([[deep_keep, *deep_arrived]], sizes, core)
    deep_sent, back = tie(deep_sent, back)
    deep_arrived = moved(deep_sent, sizes, 0)
    input_grad, grad_mine, grad_theirs = back
    gain_grads = (
        gains_attn[0], gains_attn[1, :HD], gains_attn[2, :HD], gains_ffn[0], gains_ffn[1], gains_ffn[2],
    )
    gain_block = pack_gain_grads(gain_grads, count, rows).astype(bf16)
    normed = saved[0]
    d_theirs = weight_grad(normed, grad_theirs)
    d_theirs, grad_mine = tie(d_theirs, grad_mine)
    d_mine = weight_grad(normed, grad_mine)
    narrow = [boxed(d_mine, swap(d_theirs), sizes), boxed(gain_block, None, sizes)]
    narrow_keep, narrow_sent = fold_first(narrow, sizes, core)
    deep_arrived, narrow_sent = tie(deep_arrived, narrow_sent)
    deep_keep, deep_sent = fold_z([deep_keep, *deep_arrived], sizes)
    deep_sent, narrow_sent = tie(deep_sent, narrow_sent)
    narrow_arrived, deep_arrived = moved(narrow_sent, sizes, 1), moved_z(deep_sent, sizes)
    narrow_keep, narrow_sent = fold_middle([[narrow_keep, *narrow_arrived]], sizes, core)
    narrow_arrived = moved(narrow_sent, sizes, 0)
    deep_arrived, narrow_arrived = tie(deep_arrived, narrow_arrived)
    narrow_keep, narrow_sent = fold_z([narrow_keep, *narrow_arrived], sizes)
    narrow_arrived = moved_z(narrow_sent, sizes)
    early = jnp.concatenate([total([wide_keep, *wide_arrived]), total([deep_keep, *deep_arrived])], axis=1)
    early_theirs = swap(early)

    def shard(mine, theirs, start, width):
        return in_order(core, mine[:, start : start + width], theirs[:, start : start + width])

    starts = ((0, hidden), (hidden, hidden), (2 * hidden, hidden), (3 * hidden, half))
    shards = [shard(early, early_theirs, *place) for place in starts]
    shards, narrow_arrived = tie(shards, narrow_arrived)
    narrow = total([narrow_keep, *narrow_arrived])
    narrow_theirs = swap(narrow)
    keyval = shard(narrow, narrow_theirs, half, HD)
    gain_sums = narrow[:, half + HD :] + narrow_theirs[:, half + HD :]
    return (
        outputs,
        input_grad,
        shard(narrow, narrow_theirs, 0, half),
        keyval[:, :HD],
        keyval[:, HD:],
        shards[3].T,
        shards[0],
        shards[1],
        shards[2].T,
    ) + tuple(gain_sums[:size, i] for i, size in enumerate(gain_rows))


def solution(mesh):
    sizes = factors(mesh.shape["fsdp"])
    in_specs = (
        P(None, ("fsdp", "dp"), None),
        P(None, ("fsdp", "dp"), None),
        P(),
        P(),
        P("fsdp", None),
        P("fsdp", None),
        P("fsdp", None),
        P(None, "fsdp"),
        P("fsdp", None),
        P("fsdp", None),
        P(None, "fsdp"),
        P("fsdp"),
        P("fsdp"),
        P("fsdp"),
        P("fsdp"),
        P("fsdp"),
        P("fsdp"),
    )
    out_specs = (
        P(None, ("fsdp", "dp"), None),
        P(None, ("fsdp", "dp"), None),
        P("fsdp", None),
        P("fsdp", None),
        P("fsdp", None),
        P(None, "fsdp"),
        P("fsdp", None),
        P("fsdp", None),
        P(None, "fsdp"),
        P("fsdp"),
        P("fsdp"),
        P("fsdp"),
        P("fsdp"),
        P("fsdp"),
        P("fsdp"),
    )
    return jax.shard_map(functools.partial(local, sizes), mesh=mesh, in_specs=in_specs, out_specs=out_specs, check_vma=False)
```
